128 devices in a mesh: gz: 8 (over y, core), xy: 16 (over x, z).
Axes of the slice: x: 4, y: 4, z: 4, core: 2. Of those that a mesh axis runs over, the one named last changes fastest.
Arguments:
- density: float32 [256, 512, 1024], P('gz', 'xy')
- uptake: float32 [256, 512, 1024], P('gz', 'xy'), may hold values from 0.5 to 50
- brick_values: bfloat16 [9216, 4096], P(('gz', 'xy'))
- brick_ids: int32 [9216], P(('gz', 'xy')), may hold values from 0 to 32767, as said below
- slot_counts: int32 [128, 9], P(('gz', 'xy')), may hold values from 0 to 8, as said below
Outputs:
- supply: float32 [256, 512, 1024], P('gz', 'xy')
- concentration: float32 [256, 512, 1024], P('gz', 'xy')
The draws below stay inside these ranges and needn't reach their ends.
Inputs may be any that keep to these rules, and one draw needn't show every extreme that they name: `brick_ids`: the slots 8 j to 8 j + 7 of each device (j = 0 to 8) name bricks of the device whose gz index differs by j // 3 - 1 and whose xy index differs by j % 3 - 1, or of the device itself where no such device exists; the first and the last brick of the grid are both named. `slot_counts`: entry j of a device counts the live slots at the start of its block j; it is 0 where block j's device does not exist, and 8 for j = 4.
All inputs are finite; a program needn't handle non-finite values.
Results may differ from the reference program's by a relative error of at most 0.0014.
Values may be sent and summed in bfloat16 or wider, within the bound.
A program may use at most 576 MiB of HBM per device.

```python
import math
import jax
import jax.numpy as jnp

CZ = 32
CX = 32
NY = 1024
EDGE = 16
CAP = 8
LEVELS = 4
NU = 2
NC = 4
BRICK = 4096
SLOTS = 72
NZ = 256
NX = 512
BZD = 2
BXD = 2
NBY = 64
NBX = 32
NBZ = 16
BPD = 256
NBRICKS = 32768
DEVICES = 128


def draw_density(key, part):
    base = jax.random.normal(key, (NZ, NX, NY), jnp.float32)
    zpos = jnp.arange(NZ, dtype=jnp.float32)[:, None, None] / NZ
    xpos = jnp.arange(NX, dtype=jnp.float32)[None, :, None] / NX
    ypos = jnp.arange(NY, dtype=jnp.float32)[None, None, :] / NY
    smooth = 0.6 * jnp.sin(2.0 * math.pi * xpos + 1.0) * jnp.cos(math.pi * zpos) + 0.3 * jnp.sin(2.0 * math.pi * ypos)
    return base + smooth


def draw_brick_values(key, part):
    noise_key = jax.random.fold_in(key, 11)
    level_key = jax.random.fold_in(key, 12)
    offsets = jax.random.uniform(level_key, (DEVICES * SLOTS, 1), jnp.float32, 0.0, 2.0)
    noise = jax.random.normal(noise_key, (DEVICES * SLOTS, BRICK), jnp.float32)
    return (noise + offsets).astype(jnp.bfloat16)


def draw_brick_ids(key, part):
    tiles = NX // CX
    slabs = NZ // CZ
    slot_index = jnp.arange(DEVICES * SLOTS, dtype=jnp.int32)
    device = slot_index // SLOTS
    direction = slot_index % SLOTS // CAP
    slab_at = device // tiles + direction // 3 - 1
    tile_at = device % tiles + direction % 3 - 1
    inside = (slab_at >= 0) & (slab_at < slabs) & (tile_at >= 0) & (tile_at < tiles)
    slab_at = jnp.where(inside, slab_at, device // tiles)
    tile_at = jnp.where(inside, tile_at, device % tiles)
    local_brick = jax.random.randint(jax.random.fold_in(key, 21), (DEVICES * SLOTS,), 0, BPD).astype(jnp.int32)
    local_brick = jnp.where(slot_index == 4 * CAP, 0, local_brick)
    local_brick = jnp.where(slot_index == (DEVICES - 1) * SLOTS + 4 * CAP, BPD - 1, local_brick)
    brick_z = local_brick // (BXD * NBY)
    brick_x = local_brick // NBY % BXD
    brick_y = local_brick % NBY
    global_id = ((slab_at * BZD + brick_z) * NBX + tile_at * BXD + brick_x) * NBY + brick_y
    return global_id.astype(jnp.int32)


def draw_slot_counts(key, part):
    tiles = NX // CX
    slabs = NZ // CZ
    counts = jax.random.randint(jax.random.fold_in(key, 31), (DEVICES, 9), 0, CAP + 1).astype(jnp.int32)
    device = jnp.arange(DEVICES, dtype=jnp.int32)[:, None]
    direction = jnp.arange(9, dtype=jnp.int32)[None, :]
    slab_at = device // tiles + direction // 3 - 1
    tile_at = device % tiles + direction % 3 - 1
    inside = (slab_at >= 0) & (slab_at < slabs) & (tile_at >= 0) & (tile_at < tiles)
    counts = jnp.where(direction == 4, CAP, counts)
    return jnp.where(inside, counts, 0).astype(jnp.int32)


def shard_levels(stream_key, shape, pieces, least, largest):
    def one(axis_at, blocks):
        heights = jax.random.uniform(jax.random.fold_in(jax.random.fold_in(stream_key, 6), axis_at), (blocks,), jnp.float32, least / len(pieces), largest / len(pieces))
        return jnp.repeat(jnp.exp(heights), shape[axis_at] // blocks).reshape((-1,) + (1,) * (len(shape) - axis_at - 1))

    level = one(*pieces[0])
    for cut in pieces[1:]:
        level = level * one(*cut)
    return level


def setup_inputs(seed: int = 0) -> dict:
    keys = jax.random.split(jax.random.key(seed), 6)
    return {
        "density": draw_density(jax.random.fold_in(keys[5], 71), 0),
        "uptake": jnp.clip(jnp.exp(math.log(50.0) - 4.6051702 * jax.random.uniform(keys[1], (NZ, NX, NY), jnp.float32) ** shard_levels(keys[1], (NZ, NX, NY), ((0, 8), (1, 16)), -0.2, 0.2)), 0.5, 50.0),
        "brick_values": draw_brick_values(jax.random.fold_in(keys[5], 71), 0),
        "brick_ids": draw_brick_ids(jax.random.fold_in(keys[5], 71), 0),
        "slot_counts": draw_slot_counts(jax.random.fold_in(keys[5], 71), 0),
    }


KAPPA = 32.0
OMEGA = 0.8


def neighbours(padded, values):
    y_padded = jnp.pad(values, ((0, 0), (0, 0), (1, 1)))
    summed = padded[2:, 1:-1] + padded[:-2, 1:-1]
    summed = summed + padded[1:-1, 2:] + padded[1:-1, :-2]
    summed = summed + y_padded[:, :, 2:] + y_padded[:, :, :-2]
    return summed


def operate(values, diagonal, spread):
    padded = jnp.pad(values, ((1, 1), (1, 1), (0, 0)))
    return diagonal * values - spread * neighbours(padded, values)


def smooth_once(values, source, diagonal, spread):
    return values + OMEGA * (source - operate(values, diagonal, spread)) / diagonal


def shrink(values):
    zsize, xsize, ysize = values.shape
    return values.reshape(zsize // 2, 2, xsize // 2, 2, ysize // 2, 2).mean(axis=(1, 3, 5))


def expand(values):
    return jnp.repeat(jnp.repeat(jnp.repeat(values, 2, 0), 2, 1), 2, 2)


def descend(level_index, source, start, rates):
    spread = KAPPA / 4.0 ** level_index
    diagonal = 1.0 + rates + 6.0 * spread
    estimate = start
    if level_index == LEVELS - 1:
        for repeat in range(NC):
            estimate = smooth_once(estimate, source, diagonal, spread)
        return estimate
    for repeat in range(NU):
        estimate = smooth_once(estimate, source, diagonal, spread)
    remainder = source - operate(estimate, diagonal, spread)
    coarser = shrink(remainder)
    update = descend(level_index + 1, coarser, jnp.zeros_like(coarser), shrink(rates))
    estimate = estimate + expand(update)
    for repeat in range(NU):
        estimate = smooth_once(estimate, source, diagonal, spread)
    return estimate


def reference(density, uptake, brick_values, brick_ids, slot_counts):
    values = brick_values.astype(jnp.float32)
    slot_index = jnp.arange(DEVICES * SLOTS, dtype=jnp.int32)
    owners = slot_index // SLOTS
    within = slot_index % SLOTS
    is_live = (within % CAP) < slot_counts[owners, within // CAP]
    values = jnp.where(is_live[:, None], values, 0.0)
    bricks = jnp.zeros((NBRICKS, BRICK), jnp.float32).at[brick_ids].add(values)
    secretion = bricks.reshape(NBZ, NBX, NBY, EDGE, EDGE, EDGE).transpose(0, 3, 1, 4, 2, 5).reshape(NZ, NX, NY)
    supply = density + secretion
    concentration = descend(0, supply, density, uptake)
    return supply, concentration
```

```python
import jax
import jax.numpy as jnp
from jax import lax
from jax.experimental import pallas as pl
from jax.experimental.pallas import tpu as pltpu
from jax.sharding import PartitionSpec as P

CAP = 8
BRICK = 4096
SLOTS = 72
KAPPA = (32.0, 8.0, 2.0, 0.5)
OMEGA = 0.8
LANES = 128

NZ = (32, 16, 8, 4)
NX = (32, 16, 8, 4)
NK = (8, 4, 2, 1)
HALO = (1, 3, 3, 4)
NR = (32, 24, 16, 16)
ZO = (1, 4, 4, 5)
XO = (8, 11, 11, 12)
ROWS = (48, 40, 32, 32)
PLANES = tuple(n + 2 * o for n, o in zip(NZ, ZO))

FACES = ((-1, 0), (1, 0), (0, -1), (0, 1))
AROUND = tuple((dz, dx) for dz in (-1, 0, 1) for dx in (-1, 0, 1) if dz or dx)

f32 = jnp.float32
bf16 = jnp.bfloat16


def level_shape(level):
    return (PLANES[level], NK[level], ROWS[level], LANES)


def kernel(
    dens, upt, bricks, ids, counts, out_s, out_c,
    V0, V1, V2, F0, W0, U0,
    F1, W1, D1, A1, B1, C1,
    F2, W2, D2, A2, B2, C2,
    F3, W3, A3, B3,
    RT1, RT2, RS, EB, PB, PM, EM,
    BV, XA, XT, VS, VR, IS, IR, RK, MB, TB,
    load_sem, out_sem, send_sem, recv_sem,
):
    gz, xy = lax.axis_index("gz"), lax.axis_index("xy")
    nz_dev, nx_dev = lax.axis_size("gz"), lax.axis_size("xy")
    one = jnp.minimum(gz, 0)
    taken = [0]

    def exists(dz, dx):
        ok = None
        for at, d, n in ((gz, dz, nz_dev), (xy, dx, nx_dev)):
            if d:
                cond = (at + d >= 0) & (at + d < n)
                ok = cond if ok is None else ok & cond
        return ok

    def loop(n, body, unroll=1):
        def step(i, c):
            body(i)
            return c

        lax.fori_loop(0, n, step, 0, unroll=unroll)

    class Exchange:
        def __init__(self, parts):
            self.parts = []
            for d, src, dst in parts:
                self.parts.append((d, src, dst, taken[0]))
                taken[0] += 1

        def _copy(self, d, src, dst, at):
            return pltpu.make_async_remote_copy(
                src_ref=src, dst_ref=dst, send_sem=send_sem.at[at], recv_sem=recv_sem.at[at],
                device_id=(gz + d[0], xy + d[1]), device_id_type=pl.DeviceIdType.MESH,
            )

        def start(self):
            for d, src, dst, at in self.parts:
                @pl.when(exists(*d))
                def _(d=d, src=src, dst=dst, at=at):
                    self._copy(d, src, dst, at).start()

        def wait_recv(self):
            for d, src, dst, at in self.parts:
                @pl.when(exists(-d[0], -d[1]))
                def _(d=d, src=src, dst=dst, at=at):
                    self._copy(d, src, dst, at).wait_recv()

        def wait_send(self):
            for d, src, dst, at in self.parts:
                @pl.when(exists(*d))
                def _(d=d, src=src, dst=dst, at=at):
                    self._copy(d, src, dst, at).wait_send()

    def halo_exchange(level, ref, width, directions):
        def cut(d, first, n):
            if d == 0:
                return (first, n), (first, n)
            if d > 0:
                return (first + n - width, width), (first - width, width)
            return (first, width), (first + n, width)

        parts = []
        for dz, dx in directions:
            zs, zd = cut(dz, ZO[level], NZ[level])
            xs, xd = cut(dx, XO[level], NX[level])
            parts.append((
                (dz, dx),
                ref.at[pl.ds(*zs), :, pl.ds(*xs), :],
                ref.at[pl.ds(*zd), :, pl.ds(*xd), :],
            ))
        return Exchange(parts)

    def load(src, dst_of, base):
        copies = []
        for k in range(8):
            c = pltpu.make_async_copy(
                src.at[:, :, pl.ds(k * LANES, LANES)], dst_of(k), load_sem.at[base + k]
            )
            c.start()
            copies.append(c)
        return copies

    brick_load = pltpu.make_async_copy(bricks, BV, load_sem.at[16])
    brick_load.start()
    dens_loads = load(dens, lambda k: V0.at[pl.ds(1, 32), k, pl.ds(8, 32), :], 0)
    upt_loads = load(upt, lambda k: U0.at[:, k], 8)

    def clear(ref):
        shape = ref.shape[1:]
        def body(i):
            ref[i] = jnp.zeros(shape, ref.dtype)
        loop(ref.shape[0], body)

    for V in (V0, V1, V2):
        for z in (0, 33):
            V[z] = jnp.zeros((8, 48, LANES), f32)
        def edge(z, V=V):
            V[z + 1, :, 0:8, :] = jnp.zeros((8, 8, LANES), f32)
            V[z + 1, :, 40:48, :] = jnp.zeros((8, 8, LANES), f32)
        loop(32, edge)
    for ref in (F1, W1, D1, A1, B1, C1, F2, W2, D2, A2, B2, C2, F3, W3, A3, B3):
        clear(ref)
    VR[...] = jnp.zeros(VR.shape, bf16)
    IR[...] = jnp.full(IR.shape, -1, jnp.int32)
    PB[...] = jnp.zeros(PB.shape, f32)

    barrier = pltpu.get_barrier_semaphore()
    for d in AROUND:
        @pl.when(exists(*d))
        def _(d=d):
            pl.semaphore_signal(
                barrier, inc=1, device_id=(gz + d[0], xy + d[1]), device_id_type=pl.DeviceIdType.MESH
            )

    row = lax.broadcasted_iota(jnp.int32, (256, LANES), 0)
    col = lax.broadcasted_iota(jnp.int32, (256, LANES), 1)
    pair = jnp.where(row // 2 == col, 1.0, 0.0).astype(bf16)
    PM[0:256] = pair
    PM[256:512] = pair
    row = lax.broadcasted_iota(jnp.int32, (LANES, 256), 0)
    col = lax.broadcasted_iota(jnp.int32, (LANES, 256), 1)
    twice = jnp.where(col // 2 == row, 1.0, 0.0).astype(bf16)
    EM[0:128] = twice
    EM[128:256] = twice

    for j in range(9):
        for e in range(CAP):
            IS[j, e : e + 1, :] = jnp.full((1, LANES), ids[CAP * j + e], jnp.int32)
    slot = lax.broadcasted_iota(jnp.int32, (CAP, LANES), 0)
    for j in range(9):
        v = IS[j]
        local = (((v >> 11) & 1) * 2 + ((v >> 6) & 1)) * 64 + (v & 63)
        IS[j] = jnp.where(slot < counts[0, j], local, -1)

    brick_load.wait()

    def widen(k):
        v = BV[:, pl.ds(pl.multiple_of(k * LANES, LANES), LANES)].astype(f32)
        for j in range(9):
            XA[pl.ds(pl.multiple_of((j * 32 + k) * 8, 8), 8), :] = v[8 * j : 8 * j + 8]

    loop(32, widen, unroll=2)
    chunk = lax.broadcasted_iota(jnp.int32, (32, LANES), 1) // 16

    def regroup(j):
        xs = [XA[pl.ds(j * 256 + s, 32, stride=8), :] for s in range(8)]
        for p in (1, 2, 4):
            low = (chunk & p) == 0
            for s in range(8):
                if s & p == 0:
                    a, b = xs[s], xs[s | p]
                    xs[s] = jnp.where(low, a, pltpu.roll(b, 16 * p, 1))
                    xs[s | p] = jnp.where(low, pltpu.roll(a, LANES - 16 * p, 1), b)
        for t in range(8):
            XT[pl.ds(j * 256 + t, 32, stride=8), :] = xs[t]
        VS[j] = XT[pl.ds(pl.multiple_of(j * 256, 256), 256), :].astype(bf16)

    loop(9, regroup)
    VR[:, 4 * LANES : 5 * LANES] = VS[4]
    IR[4] = IS[4]

    def beside(at, n):
        return 1 + jnp.where(at > 0, 1, 0) + jnp.where(at < n - 1, 1, 0)

    pl.semaphore_wait(barrier, beside(gz, nz_dev) * beside(xy, nx_dev) - 1)

    parts = []
    for dz, dx in AROUND:
        j = (dz + 1) * 3 + dx + 1
        parts.append(((dz, dx), VS.at[j], VR.at[:, pl.ds(j * LANES, LANES)]))
        parts.append(((dz, dx), IS.at[j], IR.at[j]))
    send_bricks = Exchange(parts)
    send_bricks.start()
    started = [send_bricks]

    def send(level, ref, width, directions):
        e = halo_exchange(level, ref, width, directions)
        e.start()
        started.append(e)
        return e

    for c in dens_loads:
        c.wait()
    x_dens = send(0, V0, 1, FACES)

    for c in upt_loads:
        c.wait()

    def weights0(z):
        for k in range(8):
            W0[z, k] = (OMEGA * KAPPA[0]) / (1.0 + 6.0 * KAPPA[0] + U0[z, k])

    loop(32, weights0)

    def split(x):
        hi = x.astype(bf16)
        return hi, (x - hi.astype(f32)).astype(bf16)

    def restrict(level, planes, store, first):
        rows = NX[level] // 2
        step = max(8, rows)
        def gather(z1):
            for k, v in enumerate(planes(z1)):
                n = v.shape[0]
                RS[k, 0:n, :] = v
                s = RS[k, pl.ds(first, rows, stride=2), :] + RS[k, pl.ds(first + 1, rows, stride=2), :]
                EB[k // 2, k % 2, pl.ds(pl.multiple_of(z1 * step, step), rows), :] = s
        loop(NZ[level] // 2, gather)
        n = NZ[level] // 2 * step
        for k1 in range(NK[level] // 2):
            x = jnp.concatenate([EB[k1, 0, 0:n, :], EB[k1, 1, 0:n, :]], axis=1)
            hi, lo = split(x)
            y = jnp.dot(jnp.concatenate([hi, lo], axis=1), PM[...], preferred_element_type=f32)
            for z1 in range(NZ[level] // 2):
                store(z1, k1, y[z1 * step : z1 * step + rows])

    EB[...] = jnp.zeros(EB.shape, f32)

    def store_rates(level, D, W, RT):
        def store(z1, k1, s):
            rates = 0.125 * s
            kappa = KAPPA[level]
            d = (1.0 + 6.0 * kappa + rates) * (1.0 / kappa)
            n = NX[level]
            W[ZO[level] + z1, k1, pl.ds(XO[level], n), :] = OMEGA / d
            if D is not None:
                D[ZO[level] + z1, k1, pl.ds(XO[level], n), :] = d
            if RT is not None:
                RT[z1, k1, 0:n, :] = rates
        return store

    restrict(0, lambda z1: [U0[2 * z1, k] + U0[2 * z1 + 1, k] for k in range(8)], store_rates(1, D1, W1, RT1), 0)
    restrict(1, lambda z1: [RT1[2 * z1, k] + RT1[2 * z1 + 1, k] for k in range(4)], store_rates(2, D2, W2, RT2), 0)
    restrict(2, lambda z1: [RT2[2 * z1, k] + RT2[2 * z1 + 1, k] for k in range(2)], store_rates(3, None, W3, None), 0)
    x_w1 = send(1, W1, HALO[1], AROUND)
    x_w2 = send(2, W2, HALO[2], AROUND)
    x_w3 = send(3, W3, HALO[3], AROUND)

    send_bricks.wait_recv()
    inner = lax.broadcasted_iota(jnp.int32, (16, LANES), 0)

    def keys(j):
        for s in range(8):
            r = jnp.broadcast_to(IR[j, s : s + 1, :], (16, LANES))
            RK[pl.ds(pl.multiple_of(j * 128 + s * 16, 16), 16), :] = jnp.where(r < 0, -1, r * 16 + inner)

    loop(9, keys)
    lane = lax.broadcasted_iota(jnp.int32, (LANES, LANES), 1)

    def secrete(i):
        def one_hot(j):
            at = pl.ds(pl.multiple_of(j * 128, 128), 128)
            key = RK[at, :]
            for half in range(2):
                hit = key == lane + (i * 256 + half * 128)
                MB[at, half * 128 : half * 128 + 128] = jnp.where(hit, 1.0, 0.0).astype(bf16)
        loop(9, one_hot)
        TB[...] = jnp.dot(VR[...], MB[...], preferred_element_type=f32)
        g = i // 4
        bz, bx, kk = g // 2, g % 2, i % 4
        def place(a):
            z = bz * 16 + a
            for half in range(2):
                k = 2 * kk + half
                x = pl.multiple_of(8 + bx * 16, 8)
                t = TB[pl.ds(pl.multiple_of(a * 16, 16), 16), half * 128 : half * 128 + 128]
                s = V0[z + 1, k, pl.ds(x, 16), :] + t
                V2[z + 1, k, pl.ds(x, 16), :] = s
                F0[z, k, pl.ds(pl.multiple_of(bx * 16, 8), 16), :] = s * (1.0 / KAPPA[0])
        loop(16, place, unroll=4)

    loop(16, secrete)
    supply_out = []
    for k in range(8):
        c = pltpu.make_async_copy(
            V2.at[pl.ds(1, 32), k, pl.ds(8, 32), :], out_s.at[:, :, pl.ds(k * LANES, LANES)], out_sem.at[k]
        )
        c.start()
        supply_out.append(c)

    def neighbours(ref, z, first, n, nk):
        lane = lax.broadcasted_iota(jnp.int32, (n, LANES), 1)
        at_first, at_last = lane == 0, lane == LANES - 1
        centre = [ref[z, k, pl.ds(first, n), :] for k in range(nk)]
        up = [pltpu.roll(c, 1, 1) for c in centre]
        down = [pltpu.roll(c, LANES - 1, 1) for c in centre]
        out = []
        for k in range(nk):
            before = up[k - 1] if k else jnp.zeros_like(up[k])
            after = down[k + 1] if k < nk - 1 else jnp.zeros_like(up[k])
            s = ref[z - 1, k, pl.ds(first, n), :] + ref[z + 1, k, pl.ds(first, n), :]
            s = s + ref[z, k, pl.ds(first - 1 + one, n), :] + ref[z, k, pl.ds(first + 1 + one, n), :]
            s = s + jnp.where(at_first, before, up[k]) + jnp.where(at_last, after, down[k])
            out.append((centre[k], s))
        return out

    def sweep0(dst, src):
        def body(z):
            for k, (c, s) in enumerate(neighbours(src, z + 1, 8, 32, 8)):
                dst[z + 1, k, 8:40, :] = (1.0 - OMEGA) * c + W0[z, k] * (F0[z, k] + s)
        loop(32, body)

    def sweep(level, dst, src, F, W, reach, inside=False):
        nk, n, xo, nx = NK[level], NR[level], XO[level], NX[level]
        start = ZO[level] - reach
        def body(i):
            z = start + i
            for k, (c, s) in enumerate(neighbours(src, z, 8, n, nk)):
                v = (1.0 - OMEGA) * c + W[z, k, 8 : 8 + n, :] * (F[z, k, 8 : 8 + n, :] + s)
                if inside:
                    dst[z, k, xo : xo + nx, :] = v[xo - 8 : xo - 8 + nx]
                else:
                    dst[z, k, 8 : 8 + n, :] = v
        loop(NZ[level] + 2 * reach, body)

    def from_zero(level, dst, F, W):
        n = NR[level]
        start = ZO[level] - HALO[level]
        def body(i):
            z = start + i
            for k in range(NK[level]):
                dst[z, k, 8 : 8 + n, :] = W[z, k, 8 : 8 + n, :] * F[z, k, 8 : 8 + n, :]
        loop(NZ[level] + 2 * HALO[level], body)

    def residual0(z):
        out = []
        for k, (c, s) in enumerate(neighbours(V2, z + 1, 8, 32, 8)):
            d = (1.0 + 6.0 * KAPPA[0]) / KAPPA[0] + (1.0 / KAPPA[0]) * U0[z, k]
            out.append(F0[z, k] - d * c + s)
        return out

    def residual(level, ref, F, D):
        n = NR[level]
        def plane(z):
            z = z + ZO[level]
            return [
                F[z, k, 8 : 8 + n, :] - D[z, k, 8 : 8 + n, :] * c + s
                for k, (c, s) in enumerate(neighbours(ref, z, 8, n, NK[level]))
            ]
        return plane

    def coarse_source(level, plane, F, first):
        def planes(z1):
            return [a + b for a, b in zip(plane(2 * z1), plane(2 * z1 + 1))]
        def store(z1, k1, s):
            F[ZO[level + 1] + z1, k1, pl.ds(XO[level + 1], NX[level + 1]), :] = 0.5 * s
        restrict(level, planes, store, first)

    def prolong(level, dst, src, reach, rows):
        c = level + 1
        n = NR[c]
        base = XO[level] + 2 * (8 - XO[c])
        first = ZO[c] - 1
        def body(i):
            zc = first + i
            x = jnp.concatenate([src[zc, k, 8 : 8 + n, :] for k in range(NK[c])], axis=0)
            hi, lo = split(x)
            y = jnp.dot(jnp.concatenate([hi, lo], axis=1), EM[...], preferred_element_type=f32)
            for k in range(NK[level]):
                v = y[(k // 2) * n : (k // 2 + 1) * n, (k % 2) * 128 : (k % 2 + 1) * 128]
                PB[k, pl.ds(base, n, stride=2), :] = v
                PB[k, pl.ds(base + 1, n, stride=2), :] = v
            z = ZO[level] + 2 * (zc - ZO[c])
            lo_r, n_r = rows
            if level == 0:
                for k in range(NK[level]):
                    p = PB[k, pl.ds(lo_r, n_r), :]
                    @pl.when(i > 0)
                    def _():
                        dst[z, k, pl.ds(lo_r, n_r), :] = dst[z, k, pl.ds(lo_r, n_r), :] + p
                    @pl.when(i < NZ[c] + 1)
                    def _():
                        dst[z + 1, k, pl.ds(lo_r, n_r), :] = dst[z + 1, k, pl.ds(lo_r, n_r), :] + p
            else:
                for k in range(NK[level]):
                    p = PB[k, pl.ds(lo_r, n_r), :]
                    for dz in range(2):
                        dst[z + dz, k, pl.ds(lo_r, n_r), :] = dst[z + dz, k, pl.ds(lo_r, n_r), :] + p
        loop(NZ[c] + 2, body)

    x_dens.wait_recv()
    level0_sends = [x_dens]
    sweep0(V1, V0)
    x = send(0, V1, 1, FACES)
    level0_sends.append(x)
    for c in supply_out:
        c.wait()
    x.wait_recv()
    sweep0(V2, V1)
    x = send(0, V2, 1, FACES)
    level0_sends.append(x)
    x.wait_recv()
    coarse_source(0, residual0, F1, 0)

    x = send(1, F1, HALO[1], AROUND)
    x_w1.wait_recv()
    x.wait_recv()
    from_zero(1, A1, F1, W1)
    sweep(1, B1, A1, F1, W1, 2)
    coarse_source(1, residual(1, B1, F1, D1), F2, XO[1] - 8)

    x = send(2, F2, HALO[2], AROUND)
    x_w2.wait_recv()
    x.wait_recv()
    from_zero(2, A2, F2, W2)
    sweep(2, B2, A2, F2, W2, 2)
    coarse_source(2, residual(2, B2, F2, D2), F3, XO[2] - 8)

    x = send(3, F3, HALO[3], AROUND)
    x_w3.wait_recv()
    x.wait_recv()
    from_zero(3, A3, F3, W3)
    sweep(3, B3, A3, F3, W3, 3)
    sweep(3, A3, B3, F3, W3, 2)
    sweep(3, B3, A3, F3, W3, 1)

    prolong(2, B2, B3, 1, (8, NR[2]))
    sweep(2, A2, B2, F2, W2, 1)
    sweep(2, C2, A2, F2, W2, 0, inside=True)
    x = send(2, C2, 1, AROUND)
    x.wait_recv()

    prolong(1, B1, C2, 1, (8, NR[1]))
    sweep(1, A1, B1, F1, W1, 1)
    sweep(1, C1, A1, F1, W1, 0, inside=True)
    x = send(1, C1, 1, FACES)
    x.wait_recv()

    for e in level0_sends:
        e.wait_send()
        started.remove(e)
    prolong(0, V2, C1, 1, (0, 48))
    sweep0(V0, V2)
    x = send(0, V0, 1, FACES)
    x.wait_recv()
    sweep0(V1, V0)
    result_out = []
    for k in range(8):
        c = pltpu.make_async_copy(
            V1.at[pl.ds(1, 32), k, pl.ds(8, 32), :], out_c.at[:, :, pl.ds(k * LANES, LANES)], out_sem.at[8 + k]
        )
        c.start()
        result_out.append(c)
    for e in started:
        e.wait_send()
    for c in result_out:
        c.wait()


def scratch():
    def vmem(*shape, dtype=f32):
        return pltpu.VMEM(shape, dtype)

    v = [vmem(*level_shape(0)) for _ in range(3)]
    v += [vmem(32, 8, 32, LANES) for _ in range(3)]
    for level, count in ((1, 6), (2, 6), (3, 4)):
        v += [vmem(*level_shape(level)) for _ in range(count)]
    v += [
        vmem(16, 4, 16, LANES), vmem(8, 2, 8, LANES),
        vmem(8, 32, LANES),
        vmem(4, 2, 256, LANES),
        vmem(8, 56, LANES),
        vmem(512, LANES, dtype=bf16), vmem(256, 256, dtype=bf16),
        vmem(SLOTS, BRICK, dtype=bf16),
        vmem(9 * 256, LANES), vmem(9 * 256, LANES),
        vmem(9, 256, LANES, dtype=bf16), vmem(256, 9 * LANES, dtype=bf16),
        vmem(9, 8, LANES, dtype=jnp.int32), vmem(9, 8, LANES, dtype=jnp.int32),
        vmem(9 * LANES, LANES, dtype=jnp.int32),
        vmem(9 * LANES, 256, dtype=bf16), vmem(256, 256),
        pltpu.SemaphoreType.DMA((17,)), pltpu.SemaphoreType.DMA((16,)),
        pltpu.SemaphoreType.DMA((100,)), pltpu.SemaphoreType.DMA((100,)),
    ]
    return v


def shards(density, uptake, brick_values, brick_ids, slot_counts):
    any_space = pl.BlockSpec(memory_space=pl.ANY)
    smem = pl.BlockSpec(memory_space=pltpu.SMEM)
    return pl.pallas_call(
        kernel,
        out_shape=(
            jax.ShapeDtypeStruct(density.shape, f32),
            jax.ShapeDtypeStruct(density.shape, f32),
        ),
        in_specs=[any_space, any_space, any_space, smem, smem],
        out_specs=(any_space, any_space),
        scratch_shapes=scratch(),
        compiler_params=pltpu.CompilerParams(
            collective_id=0, has_side_effects=True, vmem_limit_bytes=62 * 1024 * 1024
        ),
        name="tissue_step",
    )(density, uptake, brick_values, brick_ids, slot_counts)


def solution(mesh):
    return jax.shard_map(
        shards,
        mesh=mesh,
        in_specs=(
            P("gz", "xy", None),
            P("gz", "xy", None),
            P(("gz", "xy"), None),
            P(("gz", "xy")),
            P(("gz", "xy"), None),
        ),
        out_specs=(P("gz", "xy", None), P("gz", "xy", None)),
        check_vma=False,
    )
```

```python
import jax
import jax.numpy as jnp
from jax import lax
from jax.experimental import pallas as pl
from jax.experimental.pallas import tpu as pltpu
from jax.sharding import PartitionSpec as P

CAP = 8
BRICK = 4096
SLOTS = 72
KAPPA = (32.0, 8.0, 2.0, 0.5)
OMEGA = 0.8
LANES = 128

NZ = (32, 16, 8, 4)
NX = (32, 16, 8, 4)
NK = (8, 4, 2, 1)
HALO = (1, 3, 3, 4)
NR = (32, 24, 16, 16)
ZO = (1, 4, 4, 5)
XO = (8, 11, 11, 12)
ROWS = (48, 40, 32, 32)
PLANES = tuple(n + 2 * o for n, o in zip(NZ, ZO))

FACES = ((-1, 0), (1, 0), (0, -1), (0, 1))
AROUND = tuple((dz, dx) for dz in (-1, 0, 1) for dx in (-1, 0, 1) if dz or dx)

f32 = jnp.float32
bf16 = jnp.bfloat16


def level_shape(level):
    return (PLANES[level], NK[level], ROWS[level], LANES)


def kernel(
    dens, upt, bricks, ids, counts, out_s, out_c,
    V0, V1, V2, F0, W0, U0,
    F1, W1, D1, A1, B1, C1,
    F2, W2, D2, A2, B2, C2,
    F3, W3, A3, B3,
    RT1, RT2, RS, EB, PB, PM, EM,
    BV, XA, XT, VS, VR, IS, IR, RK, MB, TB,
    XSD, XD, XSV, XV,
    load_sem, out_sem, send_sem, recv_sem,
):
    gz, xy = lax.axis_index("gz"), lax.axis_index("xy")
    nz_dev, nx_dev = lax.axis_size("gz"), lax.axis_size("xy")
    one = jnp.minimum(gz, 0)
    taken = [0]
    started = []

    def exists(dz, dx):
        ok = None
        for at, d, n in ((gz, dz, nz_dev), (xy, dx, nx_dev)):
            if d:
                cond = (at + d >= 0) & (at + d < n)
                ok = cond if ok is None else ok & cond
        return ok

    def loop(n, body, unroll=1):
        def step(i, c):
            body(i)
            return c

        lax.fori_loop(0, n, step, 0, unroll=unroll)

    class Exchange:
        def __init__(self, parts):
            self.parts = []
            for d, src, dst in parts:
                self.parts.append((d, src, dst, taken[0]))
                taken[0] += 1

        def _copy(self, d, src, dst, at):
            return pltpu.make_async_remote_copy(
                src_ref=src, dst_ref=dst, send_sem=send_sem.at[at], recv_sem=recv_sem.at[at],
                device_id=(gz + d[0], xy + d[1]), device_id_type=pl.DeviceIdType.MESH,
            )

        def start(self):
            for d, src, dst, at in self.parts:
                @pl.when(exists(*d))
                def _(d=d, src=src, dst=dst, at=at):
                    self._copy(d, src, dst, at).start()

        def wait_recv(self):
            for d, src, dst, at in self.parts:
                @pl.when(exists(-d[0], -d[1]))
                def _(d=d, src=src, dst=dst, at=at):
                    self._copy(d, src, dst, at).wait_recv()

        def wait_send(self):
            for d, src, dst, at in self.parts:
                @pl.when(exists(*d))
                def _(d=d, src=src, dst=dst, at=at):
                    self._copy(d, src, dst, at).wait_send()

    def halo_exchange(level, ref, width, directions):
        def cut(d, first, n):
            if d == 0:
                return (first, n), (first, n)
            if d > 0:
                return (first + n - width, width), (first - width, width)
            return (first, width), (first + n, width)

        parts = []
        for dz, dx in directions:
            zs, zd = cut(dz, ZO[level], NZ[level])
            xs, xd = cut(dx, XO[level], NX[level])
            parts.append((
                (dz, dx),
                ref.at[pl.ds(*zs), :, pl.ds(*xs), :],
                ref.at[pl.ds(*zd), :, pl.ds(*xd), :],
            ))
        return Exchange(parts)

    class Faces:
        def __init__(self, V, out, into):
            self.rows = V.reshape(34 * 8 * 48, LANES)
            self.out, self.into = out, into
            inner = pl.ds(8, 32)
            self.z = Exchange((
                ((-1, 0), V.at[1, :, inner, :], V.at[33, :, inner, :]),
                ((1, 0), V.at[32, :, inner, :], V.at[0, :, inner, :]),
            ))
            self.x = [
                Exchange([
                    ((0, dx), out.at[side, half], into.at[side, half])
                    for side, dx in ((0, -1), (1, 1))
                ])
                for half in range(2)
            ]

        def send_x(self, half):
            def pack(i):
                z = half * 16 + 2 * i + 1
                for side, row in ((0, 8), (1, 39)):
                    v = [self.rows[pl.ds((z + p) * 384 + row, 8, stride=48), :] for p in range(2)]
                    at = pl.ds(pl.multiple_of(i * 16, 16), 16)
                    self.out[side, half, at, :] = jnp.concatenate(v, axis=0).astype(self.out.dtype)
            loop(8, pack, unroll=2)
            self.x[half].start()
            started.append(self.x[half])

        def send_z(self):
            self.z.start()
            started.append(self.z)

        def take_x(self, half):
            self.x[half].wait_recv()
            def unpack(i):
                z = half * 16 + 2 * i + 1
                for side, row in ((0, 40), (1, 7)):
                    v = self.into[side, half, pl.ds(pl.multiple_of(i * 16, 16), 16), :].astype(f32)
                    for p in range(2):
                        self.rows[pl.ds((z + p) * 384 + row, 8, stride=48), :] = v[8 * p : 8 * p + 8]
            loop(8, unpack, unroll=2)

        def take_z(self):
            self.z.wait_recv()

    def load(src, dst_of, base):
        copies = []
        for k in range(8):
            c = pltpu.make_async_copy(
                src.at[:, :, pl.ds(k * LANES, LANES)], dst_of(k), load_sem.at[base + k]
            )
            c.start()
            copies.append(c)
        return copies

    brick_load = pltpu.make_async_copy(bricks, BV, load_sem.at[16])
    brick_load.start()
    dens_loads = load(dens, lambda k: V0.at[pl.ds(1, 32), k, pl.ds(8, 32), :], 0)
    upt_loads = load(upt, lambda k: U0.at[:, k], 8)

    def clear(ref):
        shape = ref.shape[1:]
        def body(i):
            ref[i] = jnp.zeros(shape, ref.dtype)
        loop(ref.shape[0], body)

    for ref in (F1, W1, C1, F2, W2, C2, F3, W3):
        clear(ref)

    barrier = pltpu.get_barrier_semaphore()
    for d in AROUND:
        @pl.when(exists(*d))
        def _(d=d):
            pl.semaphore_signal(
                barrier, inc=1, device_id=(gz + d[0], xy + d[1]), device_id_type=pl.DeviceIdType.MESH
            )

    def absent(dz, dx):
        return jnp.logical_not(exists(dz, dx))

    for V in (V0, V1, V2):
        for dz, z in ((-1, 0), (1, 33)):
            @pl.when(absent(dz, 0))
            def _(V=V, z=z):
                V[z, :, 8:40, :] = jnp.zeros((8, 32, LANES), f32)
    for ref in (XD, XV):
        for side, dx in ((0, 1), (1, -1)):
            @pl.when(absent(0, dx))
            def _(ref=ref, side=side):
                for e in range(ref.shape[0]):
                    ref[e, side] = jnp.zeros(ref.shape[2:], ref.dtype)
    for d in AROUND:
        j = (1 - d[0]) * 3 + 1 - d[1]
        @pl.when(absent(*d))
        def _(j=j):
            VR[:, j * LANES : (j + 1) * LANES] = jnp.zeros((256, LANES), bf16)
            IR[j] = jnp.full((CAP, LANES), -1, jnp.int32)
    for level, refs in ((1, (A1, B1)), (2, (A2, B2)), (3, (A3, B3))):
        shape = (NK[level], 8, LANES)
        for ref in refs:
            def guard(z, ref=ref, end=8 + NR[level], shape=shape):
                ref[z, :, 0:8, :] = jnp.zeros(shape, f32)
                ref[z, :, end : end + 8, :] = jnp.zeros(shape, f32)
            loop(PLANES[level], guard)
    PB[...] = jnp.zeros(PB.shape, f32)

    row = lax.broadcasted_iota(jnp.int32, (256, LANES), 0)
    col = lax.broadcasted_iota(jnp.int32, (256, LANES), 1)
    pair = jnp.where(row // 2 == col, 1.0, 0.0).astype(bf16)
    PM[0:256] = pair
    PM[256:512] = pair
    row = lax.broadcasted_iota(jnp.int32, (LANES, 256), 0)
    col = lax.broadcasted_iota(jnp.int32, (LANES, 256), 1)
    twice = jnp.where(col // 2 == row, 1.0, 0.0).astype(bf16)
    EM[0:128] = twice
    EM[128:256] = twice

    for j in range(9):
        for e in range(CAP):
            IS[j, e : e + 1, :] = jnp.full((1, LANES), ids[CAP * j + e], jnp.int32)
    slot = lax.broadcasted_iota(jnp.int32, (CAP, LANES), 0)
    for j in range(9):
        v = IS[j]
        local = (((v >> 11) & 1) * 2 + ((v >> 6) & 1)) * 64 + (v & 63)
        IS[j] = jnp.where(slot < counts[0, j], local, -1)

    brick_load.wait()

    def widen(k):
        v = BV[:, pl.ds(pl.multiple_of(k * LANES, LANES), LANES)].astype(f32)
        for j in range(9):
            XA[pl.ds(pl.multiple_of((j * 32 + k) * 8, 8), 8), :] = v[8 * j : 8 * j + 8]

    loop(32, widen, unroll=2)
    chunk = lax.broadcasted_iota(jnp.int32, (32, LANES), 1) // 16

    def regroup(j):
        xs = [XA[pl.ds(j * 256 + s, 32, stride=8), :] for s in range(8)]
        for p in (1, 2, 4):
            low = (chunk & p) == 0
            for s in range(8):
                if s & p == 0:
                    a, b = xs[s], xs[s | p]
                    xs[s] = jnp.where(low, a, pltpu.roll(b, 16 * p, 1))
                    xs[s | p] = jnp.where(low, pltpu.roll(a, LANES - 16 * p, 1), b)
        for t in range(8):
            XT[pl.ds(j * 256 + t, 32, stride=8), :] = xs[t]
        VS[j] = XT[pl.ds(pl.multiple_of(j * 256, 256), 256), :].astype(bf16)

    loop(9, regroup)
    VR[:, 4 * LANES : 5 * LANES] = VS[4]
    IR[4] = IS[4]

    def beside(at, n):
        return 1 + jnp.where(at > 0, 1, 0) + jnp.where(at < n - 1, 1, 0)

    pl.semaphore_wait(barrier, beside(gz, nz_dev) * beside(xy, nx_dev) - 1)

    parts = []
    for dz, dx in AROUND:
        j = (dz + 1) * 3 + dx + 1
        parts.append(((dz, dx), VS.at[j], VR.at[:, pl.ds(j * LANES, LANES)]))
        parts.append(((dz, dx), IS.at[j], IR.at[j]))
    send_bricks = Exchange(parts)
    send_bricks.start()
    started.append(send_bricks)

    def send(level, ref, width, directions):
        e = halo_exchange(level, ref, width, directions)
        e.start()
        started.append(e)
        return e

    for c in dens_loads:
        c.wait()
    faces = [Faces(V0, XSD.at[0], XD.at[0])]
    for e, V in enumerate((V1, V2, V0)):
        faces.append(Faces(V, XSV.at[e], XV.at[e]))
    faces[0].send_z()
    for half in range(2):
        faces[0].send_x(half)

    for c in upt_loads:
        c.wait()

    def weights0(z):
        for k in range(8):
            W0[z, k] = (OMEGA * KAPPA[0]) / (1.0 + 6.0 * KAPPA[0] + U0[z, k])

    loop(32, weights0)

    def split(x):
        hi = x.astype(bf16)
        return hi, (x - hi.astype(f32)).astype(bf16)

    def restrict(level, planes, store, first, halves=None):
        rows = NX[level] // 2
        step = max(8, rows)
        def gather(z1):
            for k, v in enumerate(planes(z1)):
                v = v if isinstance(v, list) else [v]
                n = v[0].shape[0]
                for x, part in enumerate(v):
                    RS[k, x * n : (x + 1) * n, :] = part
                s = RS[k, pl.ds(first, rows, stride=2), :] + RS[k, pl.ds(first + 1, rows, stride=2), :]
                EB[k // 2, k % 2, pl.ds(pl.multiple_of(z1 * step, step), rows), :] = s
        if halves is None:
            loop(NZ[level] // 2, gather)
        else:
            halves(gather)
        n = NZ[level] // 2 * step
        for k1 in range(NK[level] // 2):
            x = jnp.concatenate([EB[k1, 0, 0:n, :], EB[k1, 1, 0:n, :]], axis=1)
            hi, lo = split(x)
            y = jnp.dot(jnp.concatenate([hi, lo], axis=1), PM[...], preferred_element_type=f32)
            for z1 in range(NZ[level] // 2):
                store(z1, k1, y[z1 * step : z1 * step + rows])

    def store_rates(level, D, W, RT):
        def store(z1, k1, s):
            rates = 0.125 * s
            kappa = KAPPA[level]
            d = (1.0 + 6.0 * kappa + rates) * (1.0 / kappa)
            n = NX[level]
            W[ZO[level] + z1, k1, pl.ds(XO[level], n), :] = OMEGA / d
            if D is not None:
                D[ZO[level] + z1, k1, pl.ds(XO[level], n), :] = d
            if RT is not None:
                RT[z1, k1, 0:n, :] = rates
        return store

    restrict(0, lambda z1: [U0[2 * z1, k] + U0[2 * z1 + 1, k] for k in range(8)], store_rates(1, D1, W1, RT1), 0)
    restrict(1, lambda z1: [RT1[2 * z1, k] + RT1[2 * z1 + 1, k] for k in range(4)], store_rates(2, D2, W2, RT2), 0)
    restrict(2, lambda z1: [RT2[2 * z1, k] + RT2[2 * z1 + 1, k] for k in range(2)], store_rates(3, None, W3, None), 0)
    x_w1 = send(1, W1, HALO[1], AROUND)
    x_w2 = send(2, W2, HALO[2], AROUND)
    x_w3 = send(3, W3, HALO[3], AROUND)

    send_bricks.wait_recv()
    inner = lax.broadcasted_iota(jnp.int32, (16, LANES), 0)

    def keys(j):
        for s in range(8):
            r = jnp.broadcast_to(IR[j, s : s + 1, :], (16, LANES))
            RK[pl.ds(pl.multiple_of(j * 128 + s * 16, 16), 16), :] = jnp.where(r < 0, -1, r * 16 + inner)

    loop(9, keys)
    lane = lax.broadcasted_iota(jnp.int32, (LANES, LANES), 1)

    def secrete(i):
        def one_hot(j):
            at = pl.ds(pl.multiple_of(j * 128, 128), 128)
            key = RK[at, :]
            for half in range(2):
                hit = key == lane + (i * 256 + half * 128)
                MB[at, half * 128 : half * 128 + 128] = jnp.where(hit, 1.0, 0.0).astype(bf16)
        loop(9, one_hot)
        TB[...] = jnp.dot(VR[...], MB[...], preferred_element_type=f32)
        g = i // 4
        bz, bx, kk = g // 2, g % 2, i % 4
        def place(a):
            z = bz * 16 + a
            for half in range(2):
                k = 2 * kk + half
                x = pl.multiple_of(8 + bx * 16, 8)
                t = TB[pl.ds(pl.multiple_of(a * 16, 16), 16), half * 128 : half * 128 + 128]
                s = V0[z + 1, k, pl.ds(x, 16), :] + t
                V2[z + 1, k, pl.ds(x, 16), :] = s
                F0[z, k, pl.ds(pl.multiple_of(bx * 16, 8), 16), :] = s * (1.0 / KAPPA[0])
        loop(16, place, unroll=4)

    loop(16, secrete)
    supply_out = []
    for k in range(8):
        c = pltpu.make_async_copy(
            V2.at[pl.ds(1, 32), k, pl.ds(8, 32), :], out_s.at[:, :, pl.ds(k * LANES, LANES)], out_sem.at[k]
        )
        c.start()
        supply_out.append(c)

    def neighbours(ref, z, first, n, nk):
        lane = lax.broadcasted_iota(jnp.int32, (n, LANES), 1)
        at_first, at_last = lane == 0, lane == LANES - 1
        centre = [ref[z, k, pl.ds(first, n), :] for k in range(nk)]
        up = [pltpu.roll(c, 1, 1) for c in centre]
        down = [pltpu.roll(c, LANES - 1, 1) for c in centre]
        out = []
        for k in range(nk):
            before = up[k - 1] if k else jnp.zeros_like(up[k])
            after = down[k + 1] if k < nk - 1 else jnp.zeros_like(up[k])
            s = ref[z - 1, k, pl.ds(first, n), :] + ref[z + 1, k, pl.ds(first, n), :]
            s = s + ref[z, k, pl.ds(first - 1 + one, n), :] + ref[z, k, pl.ds(first + 1 + one, n), :]
            s = s + jnp.where(at_first, before, up[k]) + jnp.where(at_last, after, down[k])
            out.append((centre[k], s))
        return out

    def plane0(dst, src, z):
        for x in range(4):
            at = pl.ds(8 * x, 8)
            for k, (c, s) in enumerate(neighbours(src, z + 1, 8 + 8 * x, 8, 8)):
                dst[z + 1, k, pl.ds(8 + 8 * x, 8), :] = (1.0 - OMEGA) * c + W0[z, k, at, :] * (F0[z, k, at, :] + s)

    def sweep0(dst, src, taking, sending, store=None):
        if taking is not None:
            taking.take_x(0)
        loop(15, lambda i: plane0(dst, src, i + 1))
        if taking is not None:
            taking.take_z()
            taking.take_x(1)
        plane0(dst, src, 0)
        if store is not None:
            store(0)
        else:
            sending.send_x(0)
        plane0(dst, src, 31)
        if store is None:
            sending.send_z()
        loop(15, lambda i: plane0(dst, src, i + 16))
        if store is not None:
            store(1)
        else:
            sending.send_x(1)

    def sweep(level, dst, src, F, W, reach, inside=False):
        nk, n, xo, nx = NK[level], NR[level], XO[level], NX[level]
        start = ZO[level] - reach
        def body(i):
            z = start + i
            for k, (c, s) in enumerate(neighbours(src, z, 8, n, nk)):
                v = (1.0 - OMEGA) * c + W[z, k, 8 : 8 + n, :] * (F[z, k, 8 : 8 + n, :] + s)
                if inside:
                    dst[z, k, xo : xo + nx, :] = v[xo - 8 : xo - 8 + nx]
                else:
                    dst[z, k, 8 : 8 + n, :] = v
        loop(NZ[level] + 2 * reach, body)

    def from_zero(level, dst, F, W):
        n = NR[level]
        start = ZO[level] - HALO[level]
        def body(i):
            z = start + i
            for k in range(NK[level]):
                dst[z, k, 8 : 8 + n, :] = W[z, k, 8 : 8 + n, :] * F[z, k, 8 : 8 + n, :]
        loop(NZ[level] + 2 * HALO[level], body)

    def residual0(z):
        out = [[] for _ in range(8)]
        for x in range(4):
            at = pl.ds(8 * x, 8)
            for k, (c, s) in enumerate(neighbours(V2, z + 1, 8 + 8 * x, 8, 8)):
                d = (1.0 + 6.0 * KAPPA[0]) / KAPPA[0] + (1.0 / KAPPA[0]) * U0[z, k, at, :]
                out[k].append(F0[z, k, at, :] - d * c + s)
        return out

    def residual(level, ref, F, D):
        n = NR[level]
        def plane(z):
            z = z + ZO[level]
            return [
                F[z, k, 8 : 8 + n, :] - D[z, k, 8 : 8 + n, :] * c + s
                for k, (c, s) in enumerate(neighbours(ref, z, 8, n, NK[level]))
            ]
        return plane

    def coarse_source(level, plane, F, first, halves=None):
        def planes(z1):
            return jax.tree.map(lambda a, b: a + b, plane(2 * z1), plane(2 * z1 + 1))
        def store(z1, k1, s):
            F[ZO[level + 1] + z1, k1, pl.ds(XO[level + 1], NX[level + 1]), :] = 0.5 * s
        restrict(level, planes, store, first, halves)

    def prolong(level, dst, src, reach, rows):
        c = level + 1
        n = NR[c]
        base = XO[level] + 2 * (8 - XO[c])
        first = ZO[c] - 1
        def body(i):
            zc = first + i
            x = jnp.concatenate([src[zc, k, 8 : 8 + n, :] for k in range(NK[c])], axis=0)
            hi, lo = split(x)
            y = jnp.dot(jnp.concatenate([hi, lo], axis=1), EM[...], preferred_element_type=f32)
            for k in range(NK[level]):
                v = y[(k // 2) * n : (k // 2 + 1) * n, (k % 2) * 128 : (k % 2 + 1) * 128]
                PB[k, pl.ds(base, n, stride=2), :] = v
                PB[k, pl.ds(base + 1, n, stride=2), :] = v
            z = ZO[level] + 2 * (zc - ZO[c])
            lo_r, n_r = rows
            if level == 0:
                for k in range(NK[level]):
                    p = PB[k, pl.ds(lo_r, n_r), :]
                    @pl.when(i > 0)
                    def _():
                        dst[z, k, pl.ds(lo_r, n_r), :] = dst[z, k, pl.ds(lo_r, n_r), :] + p
                    @pl.when(i < NZ[c] + 1)
                    def _():
                        dst[z + 1, k, pl.ds(lo_r, n_r), :] = dst[z + 1, k, pl.ds(lo_r, n_r), :] + p
            else:
                for k in range(NK[level]):
                    p = PB[k, pl.ds(lo_r, n_r), :]
                    for dz in range(2):
                        dst[z + dz, k, pl.ds(lo_r, n_r), :] = dst[z + dz, k, pl.ds(lo_r, n_r), :] + p
        loop(NZ[c] + 2, body)

    def all_supply():
        for c in supply_out:
            c.wait()

    sweep0(V1, V0, faces[0], faces[1])
    all_supply()
    sweep0(V2, V1, faces[1], faces[2])

    def halves(gather):
        faces[2].take_x(0)
        loop(7, lambda i: gather(i + 1))
        faces[2].take_z()
        faces[2].take_x(1)
        gather(0)
        loop(8, lambda i: gather(i + 8))

    coarse_source(0, residual0, F1, 0, halves)

    x = send(1, F1, HALO[1], AROUND)
    x_w1.wait_recv()
    x.wait_recv()
    from_zero(1, A1, F1, W1)
    sweep(1, B1, A1, F1, W1, 2)
    coarse_source(1, residual(1, B1, F1, D1), F2, XO[1] - 8)

    x = send(2, F2, HALO[2], AROUND)
    x_w2.wait_recv()
    x.wait_recv()
    from_zero(2, A2, F2, W2)
    sweep(2, B2, A2, F2, W2, 2)
    coarse_source(2, residual(2, B2, F2, D2), F3, XO[2] - 8)

    x = send(3, F3, HALO[3], AROUND)
    x_w3.wait_recv()
    x.wait_recv()
    from_zero(3, A3, F3, W3)
    sweep(3, B3, A3, F3, W3, 3)
    sweep(3, A3, B3, F3, W3, 2)
    sweep(3, B3, A3, F3, W3, 1)

    prolong(2, B2, B3, 1, (8, NR[2]))
    sweep(2, A2, B2, F2, W2, 1)
    sweep(2, C2, A2, F2, W2, 0, inside=True)
    x = send(2, C2, 1, AROUND)
    x.wait_recv()

    prolong(1, B1, C2, 1, (8, NR[1]))
    sweep(1, A1, B1, F1, W1, 1)
    sweep(1, C1, A1, F1, W1, 0, inside=True)
    x = send(1, C1, 1, FACES)
    x.wait_recv()

    for f in faces[:3]:
        for e in [f.z] + f.x:
            e.wait_send()
            started.remove(e)
    prolong(0, V2, C1, 1, (0, 48))
    sweep0(V0, V2, None, faces[3])
    result_out = []

    def store_result(half):
        for k in range(8):
            zs = pl.ds(16 * half, 16)
            c = pltpu.make_async_copy(
                V1.at[pl.ds(16 * half + 1, 16), k, pl.ds(8, 32), :],
                out_c.at[zs, :, pl.ds(k * LANES, LANES)],
                out_sem.at[8 + 8 * half + k],
            )
            c.start()
            result_out.append(c)

    sweep0(V1, V0, faces[3], None, store_result)
    for e in started:
        e.wait_send()
    for c in result_out:
        c.wait()


def scratch():
    def vmem(*shape, dtype=f32):
        return pltpu.VMEM(shape, dtype)

    v = [vmem(*level_shape(0)) for _ in range(3)]
    v += [vmem(32, 8, 32, LANES) for _ in range(3)]
    for level, count in ((1, 6), (2, 6), (3, 4)):
        v += [vmem(*level_shape(level)) for _ in range(count)]
    v += [
        vmem(16, 4, 16, LANES), vmem(8, 2, 8, LANES),
        vmem(8, 32, LANES),
        vmem(4, 2, 256, LANES),
        vmem(8, 56, LANES),
        vmem(512, LANES, dtype=bf16), vmem(256, 256, dtype=bf16),
        vmem(SLOTS, BRICK, dtype=bf16),
        vmem(9 * 256, LANES), vmem(9 * 256, LANES),
        vmem(9, 256, LANES, dtype=bf16), vmem(256, 9 * LANES, dtype=bf16),
        vmem(9, 8, LANES, dtype=jnp.int32), vmem(9, 8, LANES, dtype=jnp.int32),
        vmem(9 * LANES, LANES, dtype=jnp.int32),
        vmem(9 * LANES, 256, dtype=bf16), vmem(256, 256),
        vmem(1, 2, 2, 128, LANES), vmem(1, 2, 2, 128, LANES),
        vmem(3, 2, 2, 128, LANES, dtype=bf16), vmem(3, 2, 2, 128, LANES, dtype=bf16),
        pltpu.SemaphoreType.DMA((17,)), pltpu.SemaphoreType.DMA((24,)),
        pltpu.SemaphoreType.DMA((100,)), pltpu.SemaphoreType.DMA((100,)),
    ]
    return v


def shards(density, uptake, brick_values, brick_ids, slot_counts):
    any_space = pl.BlockSpec(memory_space=pl.ANY)
    smem = pl.BlockSpec(memory_space=pltpu.SMEM)
    return pl.pallas_call(
        kernel,
        out_shape=(
            jax.ShapeDtypeStruct(density.shape, f32),
            jax.ShapeDtypeStruct(density.shape, f32),
        ),
        in_specs=[any_space, any_space, any_space, smem, smem],
        out_specs=(any_space, any_space),
        scratch_shapes=scratch(),
        compiler_params=pltpu.CompilerParams(
            collective_id=0, has_side_effects=True, vmem_limit_bytes=62 * 1024 * 1024
        ),
        name="tissue_step",
    )(density, uptake, brick_values, brick_ids, slot_counts)


def solution(mesh):
    return jax.shard_map(
        shards,
        mesh=mesh,
        in_specs=(
            P("gz", "xy", None),
            P("gz", "xy", None),
            P(("gz", "xy"), None),
            P(("gz", "xy")),
            P(("gz", "xy"), None),
        ),
        out_specs=(P("gz", "xy", None), P("gz", "xy", None)),
        check_vma=False,
    )
```

```python
import jax
import jax.numpy as jnp
from jax import lax
from jax.experimental import pallas as pl
from jax.experimental.pallas import tpu as pltpu
from jax.sharding import PartitionSpec as P

CAP = 8
BRICK = 4096
SLOTS = 72
KAPPA = (32.0, 8.0, 2.0, 0.5)
OMEGA = 0.8
LANES = 128

NZ = (32, 16, 8, 4)
NX = (32, 16, 8, 4)
NK = (8, 4, 2, 1)
HALO = (1, 4, 5, 5)
NR = (32, 24, 24, 16)
ZO = (1, 5, 6, 6)
XO = (8, 12, 13, 13)
ROWS = (48, 40, 40, 32)
PLANES = tuple(n + 2 * o for n, o in zip(NZ, ZO))

FACES = ((-1, 0), (1, 0), (0, -1), (0, 1))
FAR = ((-2, 0), (2, 0), (0, -2), (0, 2)) + tuple(
    (a * sz, b * sx) for a, b in ((1, 2), (2, 1)) for sz in (-1, 1) for sx in (-1, 1)
)
AROUND = tuple((dz, dx) for dz in (-1, 0, 1) for dx in (-1, 0, 1) if dz or dx)

f32 = jnp.float32
bf16 = jnp.bfloat16


def level_shape(level):
    return (PLANES[level], NK[level], ROWS[level], LANES)


def kernel(
    dens, upt, bricks, ids, counts, out_s, out_c,
    V0, V1, V2, F0, W0, U0,
    F1, W1, D1, A1, B1,
    F2, W2, D2, A2, B2,
    F3, W3, A3, B3,
    RT1, RT2, EB, PM, EM,
    BV, XX, VS, VR, IS, IR, RK, MB, TB,
    XSD, XD, XSV, XV,
    load_sem, out_sem, send_sem, recv_sem,
):
    gz, xy = lax.axis_index("gz"), lax.axis_index("xy")
    nz_dev, nx_dev = lax.axis_size("gz"), lax.axis_size("xy")
    one = jnp.minimum(gz, 0)
    taken = [0]
    started = []

    def exists(dz, dx):
        ok = None
        for at, d, n in ((gz, dz, nz_dev), (xy, dx, nx_dev)):
            if d:
                cond = (at + d >= 0) & (at + d < n)
                ok = cond if ok is None else ok & cond
        return ok

    def loop(n, body, unroll=1):
        unroll = max(u for u in range(1, unroll + 1) if n % u == 0)
        def step(i, c):
            body(i)
            return c

        lax.fori_loop(0, n, step, 0, unroll=unroll)

    class Exchange:
        def __init__(self, parts):
            self.parts = []
            for d, src, dst in parts:
                self.parts.append((d, src, dst, taken[0]))
                taken[0] += 1

        def _copy(self, d, src, dst, at):
            return pltpu.make_async_remote_copy(
                src_ref=src, dst_ref=dst, send_sem=send_sem.at[at], recv_sem=recv_sem.at[at],
                device_id=(gz + d[0], xy + d[1]), device_id_type=pl.DeviceIdType.MESH,
            )

        def start(self):
            for d, src, dst, at in self.parts:
                @pl.when(exists(*d))
                def _(d=d, src=src, dst=dst, at=at):
                    self._copy(d, src, dst, at).start()

        def wait_recv(self):
            for d, src, dst, at in self.parts:
                @pl.when(exists(-d[0], -d[1]))
                def _(d=d, src=src, dst=dst, at=at):
                    self._copy(d, src, dst, at).wait_recv()

        def wait_send(self):
            for d, src, dst, at in self.parts:
                @pl.when(exists(*d))
                def _(d=d, src=src, dst=dst, at=at):
                    self._copy(d, src, dst, at).wait_send()

    def halo_exchange(level, ref, width, directions):
        def cut(d, first, n):
            if d == 0:
                return (first, n), (first, n)
            w = min(width, n) if abs(d) == 1 else width - n
            if d > 0:
                return (first + n - w, w), (first - (d - 1) * n - w, w)
            return (first, w), (first - d * n, w)

        parts = []
        for dz, dx in directions:
            zs, zd = cut(dz, ZO[level], NZ[level])
            xs, xd = cut(dx, XO[level], NX[level])
            parts.append((
                (dz, dx),
                ref.at[pl.ds(*zs), :, pl.ds(*xs), :],
                ref.at[pl.ds(*zd), :, pl.ds(*xd), :],
            ))
        return Exchange(parts)

    class Faces:
        def __init__(self, V, out, into):
            self.rows = V.reshape(34 * 8 * 48, LANES)
            self.out, self.into = out, into
            inner = pl.ds(8, 32)
            self.z = Exchange((
                ((-1, 0), V.at[1, :, inner, :], V.at[33, :, inner, :]),
                ((1, 0), V.at[32, :, inner, :], V.at[0, :, inner, :]),
            ))
            self.x = [
                Exchange([
                    ((0, dx), out.at[side, half], into.at[side, half])
                    for side, dx in ((0, -1), (1, 1))
                ])
                for half in range(2)
            ]

        def send_x(self, half):
            def pack(i):
                z = half * 16 + 2 * i + 1
                for side, row in ((0, 8), (1, 39)):
                    v = [self.rows[pl.ds((z + p) * 384 + row, 8, stride=48), :] for p in range(2)]
                    at = pl.ds(pl.multiple_of(i * 16, 16), 16)
                    self.out[side, half, at, :] = jnp.concatenate(v, axis=0).astype(self.out.dtype)
            loop(8, pack, unroll=2)
            self.x[half].start()
            started.append(self.x[half])

        def send_z(self):
            self.z.start()
            started.append(self.z)

        def take_x(self, half):
            self.x[half].wait_recv()
            def unpack(i):
                z = half * 16 + 2 * i + 1
                for side, row in ((0, 40), (1, 7)):
                    v = self.into[side, half, pl.ds(pl.multiple_of(i * 16, 16), 16), :].astype(f32)
                    for p in range(2):
                        self.rows[pl.ds((z + p) * 384 + row, 8, stride=48), :] = v[8 * p : 8 * p + 8]
            loop(8, unpack, unroll=2)

        def take_z(self):
            self.z.wait_recv()

    def load(src, dst_of, base):
        copies = []
        for k in range(8):
            c = pltpu.make_async_copy(
                src.at[:, :, pl.ds(k * LANES, LANES)], dst_of(k), load_sem.at[base + k]
            )
            c.start()
            copies.append(c)
        return copies

    brick_load = pltpu.make_async_copy(bricks, BV, load_sem.at[16])
    dens_loads = load(dens, lambda k: V0.at[pl.ds(1, 32), k, pl.ds(8, 32), :], 0)
    brick_load.start()
    upt_loads = load(upt, lambda k: U0.at[:, k], 8)

    def clear(ref):
        shape = ref.shape[1:]
        def body(i):
            ref[i] = jnp.zeros(shape, ref.dtype)
        loop(ref.shape[0], body)

    for ref in (F1, W1, F2, W2, F3, W3):
        clear(ref)

    barrier = pltpu.get_barrier_semaphore()
    for d in AROUND + FAR:
        @pl.when(exists(*d))
        def _(d=d):
            pl.semaphore_signal(
                barrier, inc=1, device_id=(gz + d[0], xy + d[1]), device_id_type=pl.DeviceIdType.MESH
            )

    def absent(dz, dx):
        return jnp.logical_not(exists(dz, dx))

    for V in (V0, V1, V2):
        for dz, z in ((-1, 0), (1, 33)):
            @pl.when(absent(dz, 0))
            def _(V=V, z=z):
                V[z, :, 8:40, :] = jnp.zeros((8, 32, LANES), f32)
    for ref in (XD, XV):
        for side, dx in ((0, 1), (1, -1)):
            @pl.when(absent(0, dx))
            def _(ref=ref, side=side):
                for e in range(ref.shape[0]):
                    ref[e, side] = jnp.zeros(ref.shape[2:], ref.dtype)
    for d in AROUND:
        j = (1 - d[0]) * 3 + 1 - d[1]
        @pl.when(absent(*d))
        def _(j=j):
            VR[:, j * LANES : (j + 1) * LANES] = jnp.zeros((256, LANES), bf16)
            IR[j] = jnp.full((CAP, LANES), -1, jnp.int32)
    for level, refs in ((1, (A1, B1)), (2, (A2, B2)), (3, (A3, B3))):
        shape = (NK[level], 8, LANES)
        for ref in refs:
            def guard(z, ref=ref, end=8 + NR[level], shape=shape):
                ref[z, :, 0:8, :] = jnp.zeros(shape, f32)
                ref[z, :, end : end + 8, :] = jnp.zeros(shape, f32)
            loop(PLANES[level], guard, 2)

    row = lax.broadcasted_iota(jnp.int32, (256, LANES), 0)
    col = lax.broadcasted_iota(jnp.int32, (256, LANES), 1)
    pair = jnp.where(row // 2 == col, 1.0, 0.0).astype(bf16)
    PM[0:256] = pair
    PM[256:512] = pair
    row = lax.broadcasted_iota(jnp.int32, (LANES, 256), 0)
    col = lax.broadcasted_iota(jnp.int32, (LANES, 256), 1)
    twice = jnp.where(col // 2 == row, 1.0, 0.0).astype(bf16)
    EM[0:128] = twice
    EM[128:256] = twice

    pl.semaphore_wait(barrier, sum(jnp.where(exists(*d), 1, 0) for d in AROUND + FAR))
    for c in dens_loads:
        c.wait()
    faces = [Faces(V0, XSD.at[0], XD.at[0])]
    for e, V in enumerate((V1, V2, V0)):
        faces.append(Faces(V, XSV.at[e], XV.at[e]))
    faces[0].send_z()
    for half in range(2):
        faces[0].send_x(half)

    for j in range(9):
        for e in range(CAP):
            IS[j, e : e + 1, :] = jnp.full((1, LANES), ids[CAP * j + e], jnp.int32)
    slot = lax.broadcasted_iota(jnp.int32, (CAP, LANES), 0)
    for j in range(9):
        v = IS[j]
        local = (((v >> 11) & 1) * 2 + ((v >> 6) & 1)) * 64 + (v & 63)
        IS[j] = jnp.where(slot < counts[0, j], local, -1)

    brick_load.wait()

    def widen(k):
        v = BV[:, pl.ds(pl.multiple_of(k * LANES, LANES), LANES)].astype(f32)
        for j in range(9):
            XX[pl.ds(pl.multiple_of((j * 32 + k) * 8, 8), 8), :] = v[8 * j : 8 * j + 8]

    loop(32, widen, 4)
    chunk = lax.broadcasted_iota(jnp.int32, (32, LANES), 1) // 16

    def regroup(j):
        xs = [XX[pl.ds(j * 256 + s, 32, stride=8), :] for s in range(8)]
        for p in (1, 2, 4):
            low = (chunk & p) == 0
            for s in range(8):
                if s & p == 0:
                    a, b = xs[s], xs[s | p]
                    xs[s] = jnp.where(low, a, pltpu.roll(b, 16 * p, 1))
                    xs[s | p] = jnp.where(low, pltpu.roll(a, LANES - 16 * p, 1), b)
        for t in range(8):
            XX[pl.ds(2304 + j * 256 + t, 32, stride=8), :] = xs[t]
        VS[j] = XX[pl.ds(pl.multiple_of(2304 + j * 256, 256), 256), :].astype(bf16)

    loop(9, regroup, 3)
    VR[:, 4 * LANES : 5 * LANES] = VS[4]
    IR[4] = IS[4]

    parts = []
    for dz, dx in AROUND:
        j = (dz + 1) * 3 + dx + 1
        parts.append(((dz, dx), VS.at[j], VR.at[:, pl.ds(j * LANES, LANES)]))
        parts.append(((dz, dx), IS.at[j], IR.at[j]))
    send_bricks = Exchange(parts)
    send_bricks.start()
    started.append(send_bricks)

    def send(level, ref, width, directions):
        e = halo_exchange(level, ref, width, directions)
        e.start()
        started.append(e)
        return e

    for c in upt_loads:
        c.wait()

    def weights0(z):
        for k in range(8):
            W0[z, k] = (OMEGA * KAPPA[0]) / (1.0 + 6.0 * KAPPA[0] + U0[z, k])

    loop(32, weights0, 2)

    def split(x):
        hi = x.astype(bf16)
        return hi, (x - hi.astype(f32)).astype(bf16)

    def restrict(level, planes, store, first, halves=None):
        rows = NX[level] // 2
        step = max(8, rows)
        nk, half = NK[level], NZ[level] // 2
        def gather(z1):
            for k, v in enumerate(planes(z1)):
                v = v if isinstance(v, list) else [v]
                n = v[0].shape[0]
                for x, part in enumerate(v):
                    XX[pl.ds(pl.multiple_of((z1 * nk + k) * 32 + x * n, 8), n), :] = part
        if halves is None:
            loop(half, gather, 2 if level == 0 else 4)
        else:
            halves(gather)
        def pair(z1):
            for k in range(nk):
                at = (z1 * nk + k) * 32 + first
                s = XX[pl.ds(at, rows, stride=2), :] + XX[pl.ds(at + 1, rows, stride=2), :]
                EB[k // 2, k % 2, pl.ds(pl.multiple_of(z1 * step, step), rows), :] = s
        loop(half, pair, 4)
        n = NZ[level] // 2 * step
        for k1 in range(NK[level] // 2):
            x = jnp.concatenate([EB[k1, 0, 0:n, :], EB[k1, 1, 0:n, :]], axis=1)
            hi, lo = split(x)
            y = jnp.dot(jnp.concatenate([hi, lo], axis=1), PM[...], preferred_element_type=f32)
            for z1 in range(NZ[level] // 2):
                store(z1, k1, y[z1 * step : z1 * step + rows])

    def store_rates(level, D, W, RT):
        def store(z1, k1, s):
            rates = 0.125 * s
            kappa = KAPPA[level]
            d = (1.0 + 6.0 * kappa + rates) * (1.0 / kappa)
            n = NX[level]
            W[ZO[level] + z1, k1, pl.ds(XO[level], n), :] = OMEGA / d
            if D is not None:
                D[ZO[level] + z1, k1, pl.ds(XO[level], n), :] = d
            if RT is not None:
                RT[z1, k1, 0:n, :] = rates
        return store

    restrict(0, lambda z1: [U0[2 * z1, k] + U0[2 * z1 + 1, k] for k in range(8)], store_rates(1, D1, W1, RT1), 0)
    restrict(1, lambda z1: [RT1[2 * z1, k] + RT1[2 * z1 + 1, k] for k in range(4)], store_rates(2, D2, W2, RT2), 0)
    restrict(2, lambda z1: [RT2[2 * z1, k] + RT2[2 * z1 + 1, k] for k in range(2)], store_rates(3, None, W3, None), 0)
    x_w1 = send(1, W1, HALO[1], AROUND)
    x_w2 = send(2, W2, HALO[2], AROUND)
    x_w3 = send(3, W3, HALO[3], AROUND + FAR)

    send_bricks.wait_recv()
    inner = lax.broadcasted_iota(jnp.int32, (16, LANES), 0)

    def keys(j):
        for s in range(8):
            r = jnp.broadcast_to(IR[j, s : s + 1, :], (16, LANES))
            RK[pl.ds(pl.multiple_of(j * 128 + s * 16, 16), 16), :] = jnp.where(r < 0, -1, r * 16 + inner)

    loop(9, keys, 3)
    lane = lax.broadcasted_iota(jnp.int32, (LANES, LANES), 1)

    def secrete(i):
        def one_hot(j):
            at = pl.ds(pl.multiple_of(j * 128, 128), 128)
            key = RK[at, :]
            for half in range(2):
                hit = key == lane + (i * 256 + half * 128)
                MB[at, half * 128 : half * 128 + 128] = jnp.where(hit, 1.0, 0.0).astype(bf16)
        loop(9, one_hot, 3)
        TB[...] = jnp.dot(VR[...], MB[...], preferred_element_type=f32)
        g = i // 4
        bz, bx, kk = g // 2, g % 2, i % 4
        def place(a):
            z = bz * 16 + a
            for half in range(2):
                k = 2 * kk + half
                x = pl.multiple_of(8 + bx * 16, 8)
                t = TB[pl.ds(pl.multiple_of(a * 16, 16), 16), half * 128 : half * 128 + 128]
                s = V0[z + 1, k, pl.ds(x, 16), :] + t
                V2[z + 1, k, pl.ds(x, 16), :] = s
                F0[z, k, pl.ds(pl.multiple_of(bx * 16, 8), 16), :] = s * (1.0 / KAPPA[0])
        loop(16, place, unroll=4)

    loop(16, secrete)
    supply_out = []
    for k in range(8):
        c = pltpu.make_async_copy(
            V2.at[pl.ds(1, 32), k, pl.ds(8, 32), :], out_s.at[:, :, pl.ds(k * LANES, LANES)], out_sem.at[k]
        )
        c.start()
        supply_out.append(c)

    def neighbours(ref, z, first, n, nk):
        lane = lax.broadcasted_iota(jnp.int32, (n, LANES), 1)
        at_first, at_last = lane == 0, lane == LANES - 1
        centre = [ref[z, k, pl.ds(first, n), :] for k in range(nk)]
        up = [pltpu.roll(c, 1, 1) for c in centre]
        down = [pltpu.roll(c, LANES - 1, 1) for c in centre]
        out = []
        for k in range(nk):
            before = up[k - 1] if k else jnp.zeros_like(up[k])
            after = down[k + 1] if k < nk - 1 else jnp.zeros_like(up[k])
            s = ref[z - 1, k, pl.ds(first, n), :] + ref[z + 1, k, pl.ds(first, n), :]
            s = s + ref[z, k, pl.ds(first - 1 + one, n), :] + ref[z, k, pl.ds(first + 1 + one, n), :]
            s = s + jnp.where(at_first, before, up[k]) + jnp.where(at_last, after, down[k])
            out.append((centre[k], s))
        return out

    def plane0(dst, src, z):
        for x in range(4):
            at = pl.ds(8 * x, 8)
            for k, (c, s) in enumerate(neighbours(src, z + 1, 8 + 8 * x, 8, 8)):
                dst[z + 1, k, pl.ds(8 + 8 * x, 8), :] = (1.0 - OMEGA) * c + W0[z, k, at, :] * (F0[z, k, at, :] + s)

    def sweep0(dst, src, taking, sending, store=None):
        if taking is not None:
            taking.take_x(0)
        loop(15, lambda i: plane0(dst, src, i + 1), 5)
        if taking is not None:
            taking.take_z()
            taking.take_x(1)
        plane0(dst, src, 0)
        if store is not None:
            store(0)
        else:
            sending.send_x(0)
        plane0(dst, src, 31)
        if store is None:
            sending.send_z()
        loop(15, lambda i: plane0(dst, src, i + 16), 5)
        if store is not None:
            store(1)
        else:
            sending.send_x(1)

    def sweep(level, dst, src, F, W, reach):
        nk, n = NK[level], NR[level]
        start = ZO[level] - reach
        def body(i):
            z = start + i
            for k, (c, s) in enumerate(neighbours(src, z, 8, n, nk)):
                dst[z, k, 8 : 8 + n, :] = (1.0 - OMEGA) * c + W[z, k, 8 : 8 + n, :] * (F[z, k, 8 : 8 + n, :] + s)
        loop(NZ[level] + 2 * reach, body, 8)

    def from_zero(level, dst, F, W):
        n = NR[level]
        start = ZO[level] - HALO[level]
        def body(i):
            z = start + i
            for k in range(NK[level]):
                dst[z, k, 8 : 8 + n, :] = W[z, k, 8 : 8 + n, :] * F[z, k, 8 : 8 + n, :]
        loop(NZ[level] + 2 * HALO[level], body, 4)

    def residual0(z):
        out = [[] for _ in range(8)]
        for x in range(4):
            at = pl.ds(8 * x, 8)
            for k, (c, s) in enumerate(neighbours(V2, z + 1, 8 + 8 * x, 8, 8)):
                d = (1.0 + 6.0 * KAPPA[0]) / KAPPA[0] + (1.0 / KAPPA[0]) * U0[z, k, at, :]
                out[k].append(F0[z, k, at, :] - d * c + s)
        return out

    def residual(level, ref, F, D):
        n = NR[level]
        def plane(z):
            z = z + ZO[level]
            return [
                F[z, k, 8 : 8 + n, :] - D[z, k, 8 : 8 + n, :] * c + s
                for k, (c, s) in enumerate(neighbours(ref, z, 8, n, NK[level]))
            ]
        return plane

    def coarse_source(level, plane, F, first, halves=None):
        def planes(z1):
            return jax.tree.map(lambda a, b: a + b, plane(2 * z1), plane(2 * z1 + 1))
        def store(z1, k1, s):
            F[ZO[level + 1] + z1, k1, pl.ds(XO[level + 1], NX[level + 1]), :] = 0.5 * s
        restrict(level, planes, store, first, halves)

    def prolong(level, dst, src, reach, buf, block):
        c = level + 1
        n, nk = NR[c], NK[level]
        base = XO[level] + 2 * (8 - XO[c])
        first, count = ZO[c] - reach, NZ[c] + 2 * reach
        def spread(i):
            x = jnp.concatenate([src[first + i, k, 8 : 8 + n, :] for k in range(NK[c])], axis=0)
            y = jnp.dot(jnp.concatenate(split(x), axis=1), EM[...], preferred_element_type=f32)
            for k in range(nk):
                v = y[(k // 2) * n : (k // 2 + 1) * n, (k % 2) * 128 : (k % 2 + 1) * 128]
                at = (i * nk + k) * block + base
                buf[pl.ds(at, n, stride=2), :] = v
                buf[pl.ds(at + 1, n, stride=2), :] = v
        loop(count, spread, 4)
        low, rows = (0, 48) if level == 0 else (8, NR[level])
        def add(i, which=(0, 1)):
            z = ZO[level] + 2 * (i - reach)
            for k in range(nk):
                p = buf[pl.ds(pl.multiple_of((i * nk + k) * block + low, 8), rows), :]
                for dz in which:
                    dst[z + dz, k, low : low + rows, :] = dst[z + dz, k, low : low + rows, :] + p
        if level == 0:
            add(0, (1,))
            loop(count - 2, lambda i: add(i + 1), 2)
            add(count - 1, (0,))
        else:
            loop(count, add, 2)

    def all_supply():
        for c in supply_out:
            c.wait()

    sweep0(V1, V0, faces[0], faces[1])
    all_supply()
    sweep0(V2, V1, faces[1], faces[2])

    def halves(gather):
        faces[2].take_x(0)
        loop(6, lambda i: gather(i + 1), 3)
        faces[2].take_z()
        faces[2].take_x(1)
        gather(0)
        gather(7)
        loop(8, lambda i: gather(i + 8), 4)

    coarse_source(0, residual0, F1, 0, halves)

    x = send(1, F1, HALO[1], AROUND)
    x_w1.wait_recv()
    x.wait_recv()
    from_zero(1, A1, F1, W1)
    sweep(1, B1, A1, F1, W1, 3)
    coarse_source(1, residual(1, B1, F1, D1), F2, XO[1] - 8)

    x = send(2, F2, HALO[2], AROUND)
    x_w2.wait_recv()
    x.wait_recv()
    from_zero(2, A2, F2, W2)
    sweep(2, B2, A2, F2, W2, 4)
    coarse_source(2, residual(2, B2, F2, D2), F3, XO[2] - 8)

    x = send(3, F3, HALO[3], AROUND + FAR)
    x_w3.wait_recv()
    x.wait_recv()
    from_zero(3, A3, F3, W3)
    sweep(3, B3, A3, F3, W3, 4)
    sweep(3, A3, B3, F3, W3, 3)
    sweep(3, B3, A3, F3, W3, 2)

    prolong(2, B2, B3, 2, XX, 64)
    sweep(2, A2, B2, F2, W2, 3)
    sweep(2, B2, A2, F2, W2, 2)

    prolong(1, B1, B2, 2, XX, 64)
    sweep(1, A1, B1, F1, W1, 2)
    sweep(1, B1, A1, F1, W1, 1)

    for f in faces[:3]:
        for e in [f.z] + f.x:
            e.wait_send()
            started.remove(e)
    prolong(0, V2, B1, 1, faces[1].rows, 48)
    sweep0(V0, V2, None, faces[3])
    result_out = []

    def store_result(half):
        for k in range(8):
            zs = pl.ds(16 * half, 16)
            c = pltpu.make_async_copy(
                V1.at[pl.ds(16 * half + 1, 16), k, pl.ds(8, 32), :],
                out_c.at[zs, :, pl.ds(k * LANES, LANES)],
                out_sem.at[8 + 8 * half + k],
            )
            c.start()
            result_out.append(c)

    sweep0(V1, V0, faces[3], None, store_result)
    for e in started:
        e.wait_send()
    for c in result_out:
        c.wait()


def scratch():
    def vmem(*shape, dtype=f32):
        return pltpu.VMEM(shape, dtype)

    v = [vmem(*level_shape(0)) for _ in range(3)]
    v += [vmem(32, 8, 32, LANES) for _ in range(3)]
    for level, count in ((1, 5), (2, 5), (3, 4)):
        v += [vmem(*level_shape(level)) for _ in range(count)]
    v += [
        vmem(16, 4, 16, LANES), vmem(8, 2, 8, LANES),
        vmem(4, 2, 256, LANES),
        vmem(512, LANES, dtype=bf16), vmem(256, 256, dtype=bf16),
        vmem(SLOTS, BRICK, dtype=bf16),
        vmem(18 * 256, LANES),
        vmem(9, 256, LANES, dtype=bf16), vmem(256, 9 * LANES, dtype=bf16),
        vmem(9, 8, LANES, dtype=jnp.int32), vmem(9, 8, LANES, dtype=jnp.int32),
        vmem(9 * LANES, LANES, dtype=jnp.int32),
        vmem(9 * LANES, 256, dtype=bf16), vmem(256, 256),
        vmem(1, 2, 2, 128, LANES), vmem(1, 2, 2, 128, LANES),
        vmem(3, 2, 2, 128, LANES, dtype=bf16), vmem(3, 2, 2, 128, LANES, dtype=bf16),
        pltpu.SemaphoreType.DMA((17,)), pltpu.SemaphoreType.DMA((24,)),
        pltpu.SemaphoreType.DMA((120,)), pltpu.SemaphoreType.DMA((120,)),
    ]
    return v


def shards(density, uptake, brick_values, brick_ids, slot_counts):
    any_space = pl.BlockSpec(memory_space=pl.ANY)
    smem = pl.BlockSpec(memory_space=pltpu.SMEM)
    return pl.pallas_call(
        kernel,
        out_shape=(
            jax.ShapeDtypeStruct(density.shape, f32),
            jax.ShapeDtypeStruct(density.shape, f32),
        ),
        in_specs=[any_space, any_space, any_space, smem, smem],
        out_specs=(any_space, any_space),
        scratch_shapes=scratch(),
        compiler_params=pltpu.CompilerParams(
            collective_id=0, has_side_effects=True, vmem_limit_bytes=62 * 1024 * 1024
        ),
        name="tissue_step",
    )(density, uptake, brick_values, brick_ids, slot_counts)


def solution(mesh):
    return jax.shard_map(
        shards,
        mesh=mesh,
        in_specs=(
            P("gz", "xy", None),
            P("gz", "xy", None),
            P(("gz", "xy"), None),
            P(("gz", "xy")),
            P(("gz", "xy"), None),
        ),
        out_specs=(P("gz", "xy", None), P("gz", "xy", None)),
        check_vma=False,
    )
```

```python
import jax
import jax.numpy as jnp
from jax import lax
from jax.experimental import pallas as pl
from jax.experimental.pallas import tpu as pltpu
from jax.sharding import PartitionSpec as P

CAP = 8
BRICK = 4096
SLOTS = 72
KAPPA = (32.0, 8.0, 2.0, 0.5)
OMEGA = 0.8
LANES = 128

NZ = (32, 16, 8, 4)
NX = (32, 16, 8, 4)
NK = (8, 4, 2, 1)
HALO = (1, 4, 5, 5)
NR = (32, 24, 24, 16)
ZO = (1, 5, 6, 6)
XO = (8, 12, 13, 13)
ROWS = (48, 40, 40, 32)
PLANES = tuple(n + 2 * o for n, o in zip(NZ, ZO))

FACES = ((-1, 0), (1, 0), (0, -1), (0, 1))
FAR = ((-2, 0), (2, 0), (0, -2), (0, 2)) + tuple(
    (a * sz, b * sx) for a, b in ((1, 2), (2, 1)) for sz in (-1, 1) for sx in (-1, 1)
)
AROUND = tuple((dz, dx) for dz in (-1, 0, 1) for dx in (-1, 0, 1) if dz or dx)

f32 = jnp.float32
bf16 = jnp.bfloat16


def level_shape(level):
    return (PLANES[level], NK[level], ROWS[level], LANES)


def kernel(
    dens, upt, bricks, ids, counts, out_s, out_c,
    V0, V1, V2, F0, W0, U0,
    F1, W1, D1, A1, B1,
    F2, W2, D2, A2, B2,
    F3, W3, A3, B3,
    RT1, RT2, EB, PM, EM,
    BV, XX, VS, VR, VG, IS, IR, RK, MB, TB,
    XSD, XD, XSV, XV, PK, LK,
    load_sem, out_sem, send_sem, recv_sem,
):
    gz, xy = lax.axis_index("gz"), lax.axis_index("xy")
    nz_dev, nx_dev = lax.axis_size("gz"), lax.axis_size("xy")
    one = jnp.minimum(gz, 0)
    taken = [0]
    started = []

    def exists(dz, dx):
        ok = None
        for at, d, n in ((gz, dz, nz_dev), (xy, dx, nx_dev)):
            if d:
                cond = (at + d >= 0) & (at + d < n)
                ok = cond if ok is None else ok & cond
        return ok

    def loop(n, body, unroll=1):
        unroll = max(u for u in range(1, unroll + 1) if n % u == 0)
        def step(i, c):
            body(i)
            return c

        lax.fori_loop(0, n, step, 0, unroll=unroll)

    class Exchange:
        def __init__(self, parts):
            self.parts = []
            for d, src, dst in parts:
                self.parts.append((d, src, dst, taken[0]))
                taken[0] += 1

        def _copy(self, d, src, dst, at):
            return pltpu.make_async_remote_copy(
                src_ref=src, dst_ref=dst, send_sem=send_sem.at[at], recv_sem=recv_sem.at[at],
                device_id=(gz + d[0], xy + d[1]), device_id_type=pl.DeviceIdType.MESH,
            )

        def start(self):
            for d, src, dst, at in self.parts:
                @pl.when(exists(*d))
                def _(d=d, src=src, dst=dst, at=at):
                    self._copy(d, src, dst, at).start()

        def wait_recv(self):
            for d, src, dst, at in self.parts:
                @pl.when(exists(-d[0], -d[1]))
                def _(d=d, src=src, dst=dst, at=at):
                    self._copy(d, src, dst, at).wait_recv()

        def wait_send(self):
            for d, src, dst, at in self.parts:
                @pl.when(exists(*d))
                def _(d=d, src=src, dst=dst, at=at):
                    self._copy(d, src, dst, at).wait_send()

    def halo_exchange(level, ref, width, directions):
        def cut(d, first, n):
            if d == 0:
                return (first, n), (first, n)
            w = min(width, n) if abs(d) == 1 else width - n
            if d > 0:
                return (first + n - w, w), (first - (d - 1) * n - w, w)
            return (first, w), (first - d * n, w)

        parts = []
        for dz, dx in directions:
            zs, zd = cut(dz, ZO[level], NZ[level])
            xs, xd = cut(dx, XO[level], NX[level])
            parts.append((
                (dz, dx),
                ref.at[pl.ds(*zs), :, pl.ds(*xs), :],
                ref.at[pl.ds(*zd), :, pl.ds(*xd), :],
            ))
        return Exchange(parts)

    class Faces:
        def __init__(self, V, out, into):
            self.rows = V.reshape(34 * 8 * 48, LANES)
            self.out, self.into = out, into
            inner = pl.ds(8, 32)
            self.z = Exchange((
                ((-1, 0), V.at[1, :, inner, :], V.at[33, :, inner, :]),
                ((1, 0), V.at[32, :, inner, :], V.at[0, :, inner, :]),
            ))
            self.x = [
                Exchange([
                    ((0, dx), out.at[side, half], into.at[side, half])
                    for side, dx in ((0, -1), (1, 1))
                ])
                for half in range(2)
            ]

        def send_x(self, half):
            def pack(i):
                z = half * 16 + 2 * i + 1
                for side, row in ((0, 8), (1, 39)):
                    v = [self.rows[pl.ds((z + p) * 384 + row, 8, stride=48), :] for p in range(2)]
                    at = pl.ds(pl.multiple_of(i * 16, 16), 16)
                    self.out[side, half, at, :] = jnp.concatenate(v, axis=0).astype(self.out.dtype)
            loop(8, pack, unroll=2)
            self.x[half].start()
            started.append(self.x[half])

        def send_z(self):
            self.z.start()
            started.append(self.z)

        def take_x(self, half):
            self.x[half].wait_recv()
            def unpack(i):
                z = half * 16 + 2 * i + 1
                for side, row in ((0, 40), (1, 7)):
                    v = self.into[side, half, pl.ds(pl.multiple_of(i * 16, 16), 16), :].astype(f32)
                    for p in range(2):
                        self.rows[pl.ds((z + p) * 384 + row, 8, stride=48), :] = v[8 * p : 8 * p + 8]
            loop(8, unpack, unroll=2)

        def take_z(self):
            self.z.wait_recv()

    class Strips:
        def __init__(self, ref, out, into):
            self.flat = ref.reshape(PLANES[1] * NK[1] * ROWS[1], LANES)
            self.out, self.into = out, into
            self.planes = halo_exchange(1, ref, HALO[1], ((-1, 0), (1, 0)))
            self.cuts = []
            for dz, src, dst in ((-1, (0, 16), (80, 16)), (0, (0, 64), (16, 64)), (1, (48, 16), (0, 16))):
                for side, dx in ((0, -1), (1, 1)):
                    self.cuts.append(((dz, dx), side, pl.ds(*src), pl.ds(*dst)))
            self.rows = Exchange([
                (d, out.at[side, :, src, :], into.at[side, :, dst, :]) for d, side, src, dst in self.cuts
            ])

        def clear(self):
            for d, side, _, dst in self.cuts:
                @pl.when(absent(-d[0], -d[1]))
                def _(side=side, dst=dst):
                    self.into[side, :, dst, :] = jnp.zeros((4, dst.size, LANES), bf16)

        def send(self):
            for side, x in ((0, XO[1]), (1, XO[1] + 12)):
                for r in range(4):
                    v = self.flat[pl.ds(ZO[1] * 160 + x + r, 64, stride=40), :]
                    self.out[side, r] = v.astype(bf16)
            for e in (self.rows, self.planes):
                e.start()
                started.append(e)

        def take(self):
            self.planes.wait_recv()
            self.rows.wait_recv()
            for side, x in ((0, XO[1] + 16), (1, XO[1] - 4)):
                for r in range(4):
                    self.flat[pl.ds((ZO[1] - 4) * 160 + x + r, 96, stride=40), :] = self.into[side, r].astype(f32)

    def load(src, dst_of, base):
        copies = []
        for k in range(8):
            c = pltpu.make_async_copy(
                src.at[:, :, pl.ds(k * LANES, LANES)], dst_of(k), load_sem.at[base + k]
            )
            c.start()
            copies.append(c)
        return copies

    brick_load = pltpu.make_async_copy(bricks, BV, load_sem.at[16])
    dens_loads = load(dens, lambda k: V0.at[pl.ds(1, 32), k, pl.ds(8, 32), :], 0)
    brick_load.start()
    upt_loads = load(upt, lambda k: U0.at[:, k], 8)

    def clear(ref):
        shape = ref.shape[1:]
        def body(i):
            ref[i] = jnp.zeros(shape, ref.dtype)
        loop(ref.shape[0], body)

    for ref in (F1, W1, F2, W2, F3, W3):
        clear(ref)

    barrier = pltpu.get_barrier_semaphore()
    for d in AROUND + FAR:
        @pl.when(exists(*d))
        def _(d=d):
            pl.semaphore_signal(
                barrier, inc=1, device_id=(gz + d[0], xy + d[1]), device_id_type=pl.DeviceIdType.MESH
            )

    def absent(dz, dx):
        return jnp.logical_not(exists(dz, dx))

    for V in (V0, V1, V2):
        for dz, z in ((-1, 0), (1, 33)):
            @pl.when(absent(dz, 0))
            def _(V=V, z=z):
                V[z, :, 8:40, :] = jnp.zeros((8, 32, LANES), f32)
    for ref in (XD, XV):
        for side, dx in ((0, 1), (1, -1)):
            @pl.when(absent(0, dx))
            def _(ref=ref, side=side):
                for e in range(ref.shape[0]):
                    ref[e, side] = jnp.zeros(ref.shape[2:], ref.dtype)
    for d in AROUND:
        j = (1 - d[0]) * 3 + 1 - d[1]
        @pl.when(absent(*d))
        def _(j=j):
            VR[:, j * LANES : (j + 1) * LANES] = jnp.zeros((256, LANES), bf16)
            IR[j] = jnp.full((2 * CAP, LANES), -1, jnp.int32)
    strips_w, strips_f = Strips(W1, PK.at[0], LK.at[0]), Strips(F1, PK.at[1], LK.at[1])
    strips_w.clear()
    strips_f.clear()
    for level, refs in ((1, (A1, B1)), (2, (A2, B2)), (3, (A3, B3))):
        shape = (NK[level], 8, LANES)
        for ref in refs:
            def guard(z, ref=ref, end=8 + NR[level], shape=shape):
                ref[z, :, 0:8, :] = jnp.zeros(shape, f32)
                ref[z, :, end : end + 8, :] = jnp.zeros(shape, f32)
            loop(PLANES[level], guard, 2)

    row = lax.broadcasted_iota(jnp.int32, (256, LANES), 0)
    col = lax.broadcasted_iota(jnp.int32, (256, LANES), 1)
    pair = jnp.where(row // 2 == col, 1.0, 0.0).astype(bf16)
    PM[0:256] = pair
    PM[256:512] = pair
    row = lax.broadcasted_iota(jnp.int32, (LANES, 256), 0)
    col = lax.broadcasted_iota(jnp.int32, (LANES, 256), 1)
    twice = jnp.where(col // 2 == row, 1.0, 0.0).astype(bf16)
    EM[0:128] = twice
    EM[128:256] = twice

    slot = lax.broadcasted_iota(jnp.int32, (CAP, LANES), 0)
    here = slot == lax.broadcasted_iota(jnp.int32, (CAP, LANES), 1) // 16
    for j in range(9):
        for e in range(CAP):
            IS[j, e : e + 1, :] = jnp.full((1, LANES), ids[CAP * j + e], jnp.int32)
    for j in range(9):
        v = IS[j, 0:8, :]
        v = (((v >> 11) & 1) * 2 + ((v >> 6) & 1)) * 64 + (v & 63)
        v = jnp.where(slot < counts[0, j], v, -1)
        IS[j, 0:8, :] = v
        IS[j, 8:16, :] = jnp.broadcast_to(jnp.sum(jnp.where(here, v, 0), axis=0, keepdims=True), (CAP, LANES))
    IR[4] = IS[4]

    pl.semaphore_wait(barrier, sum(jnp.where(exists(*d), 1, 0) for d in AROUND + FAR))
    send_ids = Exchange([
        ((dz, dx), IS.at[(dz + 1) * 3 + dx + 1], IR.at[(dz + 1) * 3 + dx + 1]) for dz, dx in AROUND
    ])
    send_ids.start()
    started.append(send_ids)
    for c in dens_loads:
        c.wait()
    faces = [Faces(V0, XSD.at[0], XD.at[0])]
    for e, V in enumerate((V1, V2, V0)):
        faces.append(Faces(V, XSV.at[e], XV.at[e]))
    faces[0].send_z()
    for half in range(2):
        faces[0].send_x(half)

    brick_load.wait()

    def widen(k):
        v = BV[:, pl.ds(pl.multiple_of(k * LANES, LANES), LANES)].astype(f32)
        for j in range(9):
            XX[pl.ds(pl.multiple_of((j * 32 + k) * 8, 8), 8), :] = v[8 * j : 8 * j + 8]

    loop(32, widen, 4)
    chunk = lax.broadcasted_iota(jnp.int32, (32, LANES), 1) // 16

    def regroup(j):
        xs = [XX[pl.ds(j * 256 + s, 32, stride=8), :] for s in range(8)]
        for p in (1, 2, 4):
            low = (chunk & p) == 0
            for s in range(8):
                if s & p == 0:
                    a, b = xs[s], xs[s | p]
                    xs[s] = jnp.where(low, a, pltpu.roll(b, 16 * p, 1))
                    xs[s | p] = jnp.where(low, pltpu.roll(a, LANES - 16 * p, 1), b)
        for t in range(8):
            XX[pl.ds(2304 + j * 256 + t, 32, stride=8), :] = xs[t]
        VS[j] = XX[pl.ds(pl.multiple_of(2304 + j * 256, 256), 256), :].astype(bf16)

    loop(9, regroup, 3)
    VR[:, 4 * LANES : 5 * LANES] = VS[4]
    parts = []
    for dz, dx in AROUND:
        j = (dz + 1) * 3 + dx + 1
        parts.append(((dz, dx), VS.at[j], VR.at[:, pl.ds(j * LANES, LANES)]))
    send_bricks = Exchange(parts)
    send_bricks.start()
    started.append(send_bricks)

    def send(level, ref, width, directions):
        e = halo_exchange(level, ref, width, directions)
        e.start()
        started.append(e)
        return e

    for c in upt_loads:
        c.wait()

    def weights0(z):
        for k in range(8):
            W0[z, k] = (OMEGA * KAPPA[0]) / (1.0 + 6.0 * KAPPA[0] + U0[z, k])

    loop(32, weights0, 2)

    def split(x):
        hi = x.astype(bf16)
        return hi, (x - hi.astype(f32)).astype(bf16)

    def restrict(level, planes, store, first, halves=None):
        rows = NX[level] // 2
        step = max(8, rows)
        nk, half = NK[level], NZ[level] // 2
        def gather(z1):
            for k, v in enumerate(planes(z1)):
                v = v if isinstance(v, list) else [v]
                n = v[0].shape[0]
                for x, part in enumerate(v):
                    XX[pl.ds(pl.multiple_of((z1 * nk + k) * 32 + x * n, 8), n), :] = part
        if halves is None:
            loop(half, gather, 2 if level == 0 else 4)
        else:
            halves(gather)
        def pair(z1):
            for k in range(nk):
                at = (z1 * nk + k) * 32 + first
                s = XX[pl.ds(at, rows, stride=2), :] + XX[pl.ds(at + 1, rows, stride=2), :]
                EB[k // 2, k % 2, pl.ds(pl.multiple_of(z1 * step, step), rows), :] = s
        loop(half, pair, 4)
        n = NZ[level] // 2 * step
        for k1 in range(NK[level] // 2):
            x = jnp.concatenate([EB[k1, 0, 0:n, :], EB[k1, 1, 0:n, :]], axis=1)
            hi, lo = split(x)
            y = jnp.dot(jnp.concatenate([hi, lo], axis=1), PM[...], preferred_element_type=f32)
            for z1 in range(NZ[level] // 2):
                store(z1, k1, y[z1 * step : z1 * step + rows])

    def store_rates(level, D, W, RT):
        def store(z1, k1, s):
            rates = 0.125 * s
            kappa = KAPPA[level]
            d = (1.0 + 6.0 * kappa + rates) * (1.0 / kappa)
            n = NX[level]
            W[ZO[level] + z1, k1, pl.ds(XO[level], n), :] = OMEGA / d
            if D is not None:
                D[ZO[level] + z1, k1, pl.ds(XO[level], n), :] = d
            if RT is not None:
                RT[z1, k1, 0:n, :] = rates
        return store

    restrict(0, lambda z1: [U0[2 * z1, k] + U0[2 * z1 + 1, k] for k in range(8)], store_rates(1, D1, W1, RT1), 0)
    restrict(1, lambda z1: [RT1[2 * z1, k] + RT1[2 * z1 + 1, k] for k in range(4)], store_rates(2, D2, W2, RT2), 0)
    restrict(2, lambda z1: [RT2[2 * z1, k] + RT2[2 * z1 + 1, k] for k in range(2)], store_rates(3, None, W3, None), 0)
    strips_w.send()
    x_w2 = send(2, W2, HALO[2], AROUND)
    x_w3 = send(3, W3, HALO[3], AROUND + FAR)

    send_ids.wait_recv()
    inner = lax.broadcasted_iota(jnp.int32, (16, LANES), 0)
    lane = lax.broadcasted_iota(jnp.int32, (LANES, LANES), 1)

    def one_hot(j):
        for e in range(CAP):
            r = jnp.broadcast_to(IR[j, e : e + 1, :], (16, LANES))
            RK[e * 16 : e * 16 + 16, :] = jnp.where(r < 0, -1, (r & 63) * 16 + inner)
        for k in range(8):
            hit = RK[...] == lane + k * LANES
            at = pl.ds(pl.multiple_of(j * LANES, LANES), LANES)
            MB[at, k * LANES : (k + 1) * LANES] = jnp.where(hit, 1.0, 0.0).astype(bf16)

    loop(9, one_hot)
    send_bricks.wait_recv()
    for j in range(9):
        v = VR[:, j * LANES : (j + 1) * LANES]
        column = IR[j, 8:9, :] >> 6
        for g in range(4):
            mask = jnp.broadcast_to(jnp.where(column == g, 1.0, 0.0), (256, LANES)).astype(bf16)
            VG[g * 256 : (g + 1) * 256, j * LANES : (j + 1) * LANES] = v * mask

    def secrete(i):
        block = MB[:, pl.ds(pl.multiple_of(i * 256, 256), 256)]
        TB[...] = jnp.dot(VG[...], block, preferred_element_type=f32)
        def place(q):
            g = q // 16
            z = g // 2 * 16 + q % 16
            for half in range(2):
                k = 2 * i + half
                t = TB[pl.ds(pl.multiple_of(q * 16, 16), 16), half * LANES : (half + 1) * LANES]
                x = pl.ds(pl.multiple_of(8 + g % 2 * 16, 8), 16)
                s = V0[z + 1, k, x, :] + t
                V2[z + 1, k, x, :] = s
                F0[z, k, pl.ds(pl.multiple_of(g % 2 * 16, 8), 16), :] = s * (1.0 / KAPPA[0])
        loop(64, place, 8)

    loop(4, secrete)
    supply_out = []
    for k in range(8):
        c = pltpu.make_async_copy(
            V2.at[pl.ds(1, 32), k, pl.ds(8, 32), :], out_s.at[:, :, pl.ds(k * LANES, LANES)], out_sem.at[k]
        )
        c.start()
        supply_out.append(c)

    def neighbours(ref, z, first, n, nk):
        lane = lax.broadcasted_iota(jnp.int32, (n, LANES), 1)
        at_first, at_last = lane == 0, lane == LANES - 1
        centre = [ref[z, k, pl.ds(first, n), :] for k in range(nk)]
        up = [pltpu.roll(c, 1, 1) for c in centre]
        down = [pltpu.roll(c, LANES - 1, 1) for c in centre]
        out = []
        for k in range(nk):
            before = up[k - 1] if k else jnp.zeros_like(up[k])
            after = down[k + 1] if k < nk - 1 else jnp.zeros_like(up[k])
            s = ref[z - 1, k, pl.ds(first, n), :] + ref[z + 1, k, pl.ds(first, n), :]
            s = s + ref[z, k, pl.ds(first - 1 + one, n), :] + ref[z, k, pl.ds(first + 1 + one, n), :]
            s = s + jnp.where(at_first, before, up[k]) + jnp.where(at_last, after, down[k])
            out.append((centre[k], s))
        return out

    def plane0(dst, src, z):
        for x in range(4):
            at = pl.ds(8 * x, 8)
            for k, (c, s) in enumerate(neighbours(src, z + 1, 8 + 8 * x, 8, 8)):
                dst[z + 1, k, pl.ds(8 + 8 * x, 8), :] = (1.0 - OMEGA) * c + W0[z, k, at, :] * (F0[z, k, at, :] + s)

    def sweep0(dst, src, taking, sending, store=None):
        if taking is not None:
            taking.take_x(0)
        loop(15, lambda i: plane0(dst, src, i + 1), 5)
        if taking is not None:
            taking.take_z()
            taking.take_x(1)
        plane0(dst, src, 0)
        if store is not None:
            store(0)
        else:
            sending.send_x(0)
        plane0(dst, src, 31)
        if store is None:
            sending.send_z()
        loop(15, lambda i: plane0(dst, src, i + 16), 5)
        if store is not None:
            store(1)
        else:
            sending.send_x(1)

    def sweep(level, dst, src, F, W, reach):
        nk, n = NK[level], NR[level]
        start = ZO[level] - reach
        def body(i):
            z = start + i
            for k, (c, s) in enumerate(neighbours(src, z, 8, n, nk)):
                dst[z, k, 8 : 8 + n, :] = (1.0 - OMEGA) * c + W[z, k, 8 : 8 + n, :] * (F[z, k, 8 : 8 + n, :] + s)
        loop(NZ[level] + 2 * reach, body, 8)

    def from_zero(level, dst, F, W):
        n = NR[level]
        start = ZO[level] - HALO[level]
        def body(i):
            z = start + i
            for k in range(NK[level]):
                dst[z, k, 8 : 8 + n, :] = W[z, k, 8 : 8 + n, :] * F[z, k, 8 : 8 + n, :]
        loop(NZ[level] + 2 * HALO[level], body, 4)

    def residual0(z):
        out = [[] for _ in range(8)]
        for x in range(4):
            at = pl.ds(8 * x, 8)
            for k, (c, s) in enumerate(neighbours(V2, z + 1, 8 + 8 * x, 8, 8)):
                d = (1.0 + 6.0 * KAPPA[0]) / KAPPA[0] + (1.0 / KAPPA[0]) * U0[z, k, at, :]
                out[k].append(F0[z, k, at, :] - d * c + s)
        return out

    def residual(level, ref, F, D):
        n = NR[level]
        def plane(z):
            z = z + ZO[level]
            return [
                F[z, k, 8 : 8 + n, :] - D[z, k, 8 : 8 + n, :] * c + s
                for k, (c, s) in enumerate(neighbours(ref, z, 8, n, NK[level]))
            ]
        return plane

    def coarse_source(level, plane, F, first, halves=None):
        def planes(z1):
            return jax.tree.map(lambda a, b: a + b, plane(2 * z1), plane(2 * z1 + 1))
        def store(z1, k1, s):
            F[ZO[level + 1] + z1, k1, pl.ds(XO[level + 1], NX[level + 1]), :] = 0.5 * s
        restrict(level, planes, store, first, halves)

    def prolong(level, dst, src, reach, buf, block):
        c = level + 1
        n, nk = NR[c], NK[level]
        base = XO[level] + 2 * (8 - XO[c])
        first, count = ZO[c] - reach, NZ[c] + 2 * reach
        def spread(i):
            x = jnp.concatenate([src[first + i, k, 8 : 8 + n, :] for k in range(NK[c])], axis=0)
            y = jnp.dot(jnp.concatenate(split(x), axis=1), EM[...], preferred_element_type=f32)
            for k in range(nk):
                v = y[(k // 2) * n : (k // 2 + 1) * n, (k % 2) * 128 : (k % 2 + 1) * 128]
                at = (i * nk + k) * block + base
                buf[pl.ds(at, n, stride=2), :] = v
                buf[pl.ds(at + 1, n, stride=2), :] = v
        loop(count, spread, 4)
        low, rows = (0, 48) if level == 0 else (8, NR[level])
        def add(i, which=(0, 1)):
            z = ZO[level] + 2 * (i - reach)
            for k in range(nk):
                p = buf[pl.ds(pl.multiple_of((i * nk + k) * block + low, 8), rows), :]
                for dz in which:
                    dst[z + dz, k, low : low + rows, :] = dst[z + dz, k, low : low + rows, :] + p
        if level == 0:
            add(0, (1,))
            loop(count - 2, lambda i: add(i + 1), 2)
            add(count - 1, (0,))
        else:
            loop(count, add, 2)

    def all_supply():
        for c in supply_out:
            c.wait()

    sweep0(V1, V0, faces[0], faces[1])
    all_supply()
    sweep0(V2, V1, faces[1], faces[2])

    def halves(gather):
        faces[2].take_x(0)
        loop(6, lambda i: gather(i + 1), 3)
        faces[2].take_z()
        faces[2].take_x(1)
        gather(0)
        gather(7)
        loop(8, lambda i: gather(i + 8), 4)

    coarse_source(0, residual0, F1, 0, halves)

    strips_f.send()
    strips_w.take()
    strips_f.take()
    from_zero(1, A1, F1, W1)
    sweep(1, B1, A1, F1, W1, 3)
    coarse_source(1, residual(1, B1, F1, D1), F2, XO[1] - 8)

    x = send(2, F2, HALO[2], AROUND)
    x_w2.wait_recv()
    x.wait_recv()
    from_zero(2, A2, F2, W2)
    sweep(2, B2, A2, F2, W2, 4)
    coarse_source(2, residual(2, B2, F2, D2), F3, XO[2] - 8)

    x = send(3, F3, HALO[3], AROUND + FAR)
    x_w3.wait_recv()
    x.wait_recv()
    from_zero(3, A3, F3, W3)
    sweep(3, B3, A3, F3, W3, 4)
    sweep(3, A3, B3, F3, W3, 3)
    sweep(3, B3, A3, F3, W3, 2)

    prolong(2, B2, B3, 2, XX, 64)
    sweep(2, A2, B2, F2, W2, 3)
    sweep(2, B2, A2, F2, W2, 2)

    prolong(1, B1, B2, 2, XX, 64)
    sweep(1, A1, B1, F1, W1, 2)
    sweep(1, B1, A1, F1, W1, 1)

    for f in faces[:3]:
        for e in [f.z] + f.x:
            e.wait_send()
            started.remove(e)
    prolong(0, V2, B1, 1, faces[1].rows, 48)
    sweep0(V0, V2, None, faces[3])
    result_out = []

    def store_result(half):
        for k in range(8):
            zs = pl.ds(16 * half, 16)
            c = pltpu.make_async_copy(
                V1.at[pl.ds(16 * half + 1, 16), k, pl.ds(8, 32), :],
                out_c.at[zs, :, pl.ds(k * LANES, LANES)],
                out_sem.at[8 + 8 * half + k],
            )
            c.start()
            result_out.append(c)

    sweep0(V1, V0, faces[3], None, store_result)
    for e in started:
        e.wait_send()
    for c in result_out:
        c.wait()


def scratch():
    def vmem(*shape, dtype=f32):
        return pltpu.VMEM(shape, dtype)

    v = [vmem(*level_shape(0)) for _ in range(3)]
    v += [vmem(32, 8, 32, LANES) for _ in range(3)]
    for level, count in ((1, 5), (2, 5), (3, 4)):
        v += [vmem(*level_shape(level)) for _ in range(count)]
    v += [
        vmem(16, 4, 16, LANES), vmem(8, 2, 8, LANES),
        vmem(4, 2, 256, LANES),
        vmem(512, LANES, dtype=bf16), vmem(256, 256, dtype=bf16),
        vmem(SLOTS, BRICK, dtype=bf16),
        vmem(18 * 256, LANES),
        vmem(9, 256, LANES, dtype=bf16), vmem(256, 9 * LANES, dtype=bf16),
        vmem(1024, 9 * LANES, dtype=bf16),
        vmem(9, 16, LANES, dtype=jnp.int32), vmem(9, 16, LANES, dtype=jnp.int32),
        vmem(LANES, LANES, dtype=jnp.int32),
        vmem(9 * LANES, 1024, dtype=bf16), vmem(1024, 256),
        vmem(1, 2, 2, 128, LANES), vmem(1, 2, 2, 128, LANES),
        vmem(3, 2, 2, 128, LANES, dtype=bf16), vmem(3, 2, 2, 128, LANES, dtype=bf16),
        vmem(2, 2, 4, 64, LANES, dtype=bf16), vmem(2, 2, 4, 96, LANES, dtype=bf16),
        pltpu.SemaphoreType.DMA((17,)), pltpu.SemaphoreType.DMA((24,)),
        pltpu.SemaphoreType.DMA((120,)), pltpu.SemaphoreType.DMA((120,)),
    ]
    return v


def shards(density, uptake, brick_values, brick_ids, slot_counts):
    any_space = pl.BlockSpec(memory_space=pl.ANY)
    smem = pl.BlockSpec(memory_space=pltpu.SMEM)
    return pl.pallas_call(
        kernel,
        out_shape=(
            jax.ShapeDtypeStruct(density.shape, f32),
            jax.ShapeDtypeStruct(density.shape, f32),
        ),
        in_specs=[any_space, any_space, any_space, smem, smem],
        out_specs=(any_space, any_space),
        scratch_shapes=scratch(),
        compiler_params=pltpu.CompilerParams(
            collective_id=0, has_side_effects=True, vmem_limit_bytes=62 * 1024 * 1024
        ),
        name="tissue_step",
    )(density, uptake, brick_values, brick_ids, slot_counts)


def solution(mesh):
    return jax.shard_map(
        shards,
        mesh=mesh,
        in_specs=(
            P("gz", "xy", None),
            P("gz", "xy", None),
            P(("gz", "xy"), None),
            P(("gz", "xy")),
            P(("gz", "xy"), None),
        ),
        out_specs=(P("gz", "xy", None), P("gz", "xy", None)),
        check_vma=False,
    )
```
